32 devices in a mesh: vec: 4 (over y, core), space: 8 (over z, x).
Axes of the slice: x: 2, y: 2, z: 4, core: 2. Of those that a mesh axis runs over, the one named last changes fastest.
Arguments:
- tangents: float32 [16, 2, 16, 128, 128], P('vec', None, 'space'), may hold values from -16 to 16
- background: bfloat16 [3, 4, 16, 128, 128], P(None, None, 'space', 'vec'), may hold values from -4 to 4
Outputs:
- basis: float32 [16, 2, 16, 128, 128], P('vec', None, 'space')
- growth: float32 [16], replicated
The draws below stay inside these ranges and needn't reach their ends.
All inputs are finite; a program needn't handle non-finite values.
Results may differ from the reference program's by a relative error of at most 0.00045.
Values may be sent and summed in bfloat16 or wider, within the bound.
No kernel may reach another device: no remote copies, remote signals or barrier semaphores. Data moves between devices by JAX's collectives and lax.ppermute only.
A program may use at most 64 MiB of HBM per device.

```python
import jax
import jax.numpy as jnp
from jax import lax

NX = 128
LEVELS = 128
VECTORS = 16
NY = 16


def draw_tangents(key, part):
    key = jax.random.fold_in(key, 11)
    key_common, key_noise, key_mix = jax.random.split(key, 3)
    common = jax.random.truncated_normal(key_common, -4.0, 4.0, (2, NY, NX, LEVELS), jnp.float32)
    noise = jax.random.truncated_normal(key_noise, -4.0, 4.0, (VECTORS, 2, NY, NX, LEVELS), jnp.float32)
    mix = jax.random.uniform(key_mix, (VECTORS, 1, 1, 1, 1), jnp.float32, 0.3, 0.8)
    rising = 1.0 + 2.0 * jnp.arange(NY, dtype=jnp.float32) / (NY - 1)
    scale = rising.reshape(1, 1, NY, 1, 1)
    return mix * common[None] + noise * scale


def level_of(own_key, dims, shards, least, top_value):
    gain, own = 1.0, jax.random.fold_in(own_key, 6)
    for position, shards_of in shards:
        draws = jnp.exp(jax.random.uniform(jax.random.fold_in(own, position), (shards_of,), jnp.float32, least / len(shards), top_value / len(shards)))
        gain = gain * jnp.repeat(draws, dims[position] // shards_of).reshape([-1 if axis == position else 1 for axis in range(len(dims))])
    return gain


def normal_values(own_key, dims, width, most, cuts=(), held_as=jnp.bfloat16):
    values = width * jax.random.normal(own_key, dims, jnp.float32)
    if cuts:
        values = values * level_of(own_key, dims, cuts, -0.22, 0.18)
    return jnp.clip(values, -most, most).astype(held_as)


def setup_inputs(seed: int = 0) -> dict:
    streams_of = jax.random.split(jax.random.key(seed), 3)
    tangents = draw_tangents(jax.random.fold_in(streams_of[2], 71), 0)
    background = normal_values(streams_of[1], (3, 4, NY, NX, LEVELS), 1.0, 4.0, ((2, 8), (3, 4)))
    return dict(tangents=tangents, background=background)


time_step = 0.1
diffusion = 0.5

def combine(center, x_next, x_prev, y_next, y_prev, z_next, z_prev, section):
    dxf = (x_next - x_prev) * 0.5
    dyf = (y_next - y_prev) * 0.5
    dzf = (z_next - z_prev) * 0.5
    lap = x_next + x_prev + y_next + y_prev + z_next + z_prev - 6.0 * center
    speed_u = section[0]
    speed_v = section[1]
    speed_r = section[2]
    strat = section[3]
    adv = speed_u * dxf + speed_v * dyf + speed_r * dzf
    w_rate = -adv[..., 0, :, :, :] + center[..., 1, :, :, :] + diffusion * lap[..., 0, :, :, :]
    b_rate = -adv[..., 1, :, :, :] - strat * center[..., 0, :, :, :] + diffusion * lap[..., 1, :, :, :]
    return jnp.stack([w_rate, b_rate], -4)

def rates(field, section):
    center = field
    x_next = jnp.roll(center, -1, -2)
    x_prev = jnp.roll(center, 1, -2)
    y_next = jnp.roll(center, -1, -3)
    y_prev = jnp.roll(center, 1, -3)
    widths = [(0, 0)] * (center.ndim - 1) + [(1, 1)]
    zpad = jnp.pad(center, widths)
    z_next = zpad[..., 2:]
    z_prev = zpad[..., :-2]
    return combine(center, x_next, x_prev, y_next, y_prev, z_next, z_prev, section)

def reference(tangents, background):
    sections = background.astype(jnp.float32)

    def advance(vector):
        section_one = vector + time_step * rates(vector, sections[0])
        section_two = 0.75 * vector + 0.25 * (section_one + time_step * rates(section_one, sections[1]))
        return vector / 3.0 + 2.0 / 3.0 * (section_two + time_step * rates(section_two, sections[2]))
    advanced = lax.map(advance, tangents)
    flat = advanced.reshape(advanced.shape[0], -1)
    cells = flat.shape[1]
    gram = jnp.dot(flat, flat.T, precision=lax.Precision.HIGHEST) / cells
    lower = jnp.linalg.cholesky(gram)
    eye = jnp.eye(gram.shape[0], dtype=jnp.float32)
    inverse = lax.linalg.triangular_solve(lower, eye, left_side=True, lower=True)
    basis = jnp.dot(inverse, flat, precision=lax.Precision.HIGHEST).reshape(advanced.shape)
    growth = jnp.log(jnp.diagonal(lower))
    return (basis, growth)
```

```python
import functools

import jax
import jax.numpy as jnp
from jax import lax
from jax.experimental import pallas as pl
from jax.experimental.pallas import tpu as pltpu
from jax.sharding import PartitionSpec as P

time_step = 0.1
diffusion = 0.5
VM = pl.BlockSpec(memory_space=pltpu.VMEM)
SM = pl.BlockSpec(memory_space=pltpu.SMEM)
PARAMS = pltpu.CompilerParams(vmem_limit_bytes=40 * 1024 * 1024)
PAD = 8
CHUNK = 16


def stage_rows(src, first, bgs, bg_first, alpha, beta, keep, keep_first, rows, vectors, store):
    columns = src.shape[2] - 2 * PAD
    levels = src.shape[3]
    h = beta * time_step
    lane = lax.broadcasted_iota(jnp.int32, (CHUNK, levels), 1)

    def one_row(row, carry):
        at = row + first
        for x in range(0, columns, CHUNK):
            quarter, inner = divmod(x, bgs.shape[3])
            u, v, r, s = (
                bgs[bg_first + row, f, quarter, inner : inner + CHUNK, :].astype(jnp.float32)
                for f in range(4)
            )
            hu, hv, hr, hs = (0.5 * h) * u, (0.5 * h) * v, (0.5 * h) * r, h * s
            lap = diffusion * h
            xn_c, xp_c = lap - hu, lap + hu
            yn_c, yp_c = lap - hv, lap + hv
            zn_c = jnp.where(lane == levels - 1, 0.0, lap - hr)
            zp_c = jnp.where(lane == 0, 0.0, lap + hr)
            mid = beta - 6.0 * lap
            lo = PAD + x
            for vector in range(vectors):
                centers = [src[at, 2 * vector + f, lo : lo + CHUNK, :] for f in range(2)]
                for f in range(2):
                    k = 2 * vector + f
                    c = centers[f]
                    total = xn_c * src[at, k, lo + 1 : lo + 1 + CHUNK, :]
                    total += xp_c * src[at, k, lo - 1 : lo - 1 + CHUNK, :]
                    total += yn_c * src[at + 1, k, lo : lo + CHUNK, :]
                    total += yp_c * src[at - 1, k, lo : lo + CHUNK, :]
                    total += zn_c * pltpu.roll(c, levels - 1, 1)
                    total += zp_c * pltpu.roll(c, 1, 1)
                    total += mid * c
                    if f == 0:
                        total += h * centers[1]
                    else:
                        total -= hs * centers[0]
                    if alpha:
                        total += alpha * keep[row + keep_first, k, lo : lo + CHUNK, :]
                    store(row, vector, f, x, total)
        return carry

    lax.fori_loop(0, rows, one_row, 0)


def wrap(ref, columns):
    ref[:, :, PAD - 1 : PAD, :] = ref[:, :, PAD + columns - 1 : PAD + columns, :]
    ref[:, :, PAD + columns : PAD + columns + 1, :] = ref[:, :, PAD : PAD + 1, :]


def advance_kernel(me, own, up1, dn1, up2, dn2, bg0, bg2, bg13, adv, q0, q1, q2, q3, p0, p1, p2, bgs):
    vectors, _, rows, columns, _ = own.shape
    position = me[0]
    bgs[:, :, position] = bg0[...]
    bgs[:, :, position ^ 2] = bg2[...]
    bgs[:, :, position ^ 1] = bg13[0]
    bgs[:, :, position ^ 3] = bg13[1]
    for vector in range(vectors):
        for f in range(2):
            k = 2 * vector + f
            cells = slice(PAD, PAD + columns)
            p0[0, k, cells, :] = up2[vector, f].astype(jnp.float32)
            p0[7, k, cells, :] = dn2[vector, f].astype(jnp.float32)
            for row in range(2):
                p0[1 + row, k, cells, :] = up1[vector, f, row].astype(jnp.float32)
                p0[3 + row, k, cells, :] = own[vector, f, row]
                p0[5 + row, k, cells, :] = dn1[vector, f, row].astype(jnp.float32)
    wrap(p0, columns)

    def to(ref):
        def store(row, vector, f, x, value):
            ref[row, 2 * vector + f, PAD + x : PAD + x + CHUNK, :] = value

        return store

    def to_out(row, vector, f, x, value):
        adv[vector, f, row, x : x + CHUNK, :] = value

    stage_rows(p0, 1, bgs, 0, 0.0, 1.0, None, 0, 6, vectors, to(p1))
    wrap(p1, columns)
    stage_rows(p1, 1, bgs, 6, 0.75, 0.25, p0, 2, 4, vectors, to(p2))
    wrap(p2, columns)
    stage_rows(p2, 1, bgs, 10, 1.0 / 3.0, 2.0 / 3.0, p0, 3, 2, vectors, to_out)
    for b, q in enumerate((q0, q1, q2, q3)):
        part = position ^ b
        for vector in range(vectors):
            q[vector] = adv[vector, part // 2, part % 2].astype(jnp.bfloat16)


def gram_kernel(me, q0, q1, q2, q3, out, flat):
    vectors, columns, levels = q0.shape
    position = me[0]
    for b, q in enumerate((q0, q1, q2, q3)):
        block = position ^ b
        for vector in range(vectors):
            flat[block * vectors + vector] = q[vector].astype(jnp.float32)
    count = vectors * 4
    rows = flat.reshape(count * columns, levels)
    total = jnp.zeros((count, count), jnp.float32)
    for x in range(0, columns, 2):
        part = jnp.concatenate(
            [rows[pl.ds(x + i, count, stride=columns), :].astype(jnp.bfloat16) for i in range(2)], 1
        )
        total += lax.dot_general(
            part, part, (((1,), (1,)), ((), ())), preferred_element_type=jnp.float32
        )
    out[...] = total


def final_kernel(scale, me, gram, own, r1, r2, r3, basis, growth, inv):
    vectors = own.shape[0]
    count = gram.shape[0]
    position = me[0]
    row = lax.broadcasted_iota(jnp.int32, (count, 2 * count), 0)
    lane = lax.broadcasted_iota(jnp.int32, (count, 2 * count), 1)
    unit = lane - count
    column = ((unit // vectors) ^ position) * vectors + unit % vectors
    eye = jnp.where((lane >= count) & (row == column), 1.0, 0.0)
    table = jnp.concatenate([gram[...] * scale, jnp.zeros((count, count), jnp.float32)], 1) + eye
    pivots = jnp.zeros((1, count), jnp.float32)
    wide = lax.broadcasted_iota(jnp.int32, (1, count), 1)
    for k in range(count):
        pivot = table[k : k + 1, k : k + 1]
        pivots = jnp.where(wide == k, pivot, pivots)
        scaled = table[k : k + 1, :] / jnp.sqrt(pivot)
        below = jnp.where(row[:, :1] > k, table[:, k : k + 1] / jnp.sqrt(pivot), 0.0)
        table = jnp.where(row == k, scaled, table - below * scaled)
    growth[...] = 0.5 * jnp.log(pivots)
    inv[...] = table
    for first in range(0, vectors, 2):
        weights = []
        for i in range(first, first + 2):
            line = inv[pl.ds(position * vectors + i, 1), :]
            weights.append(
                [
                    jnp.broadcast_to(line[:, count + j : count + j + 1], (8, own.shape[4]))
                    for j in range(count)
                ]
            )
        for f in range(own.shape[1]):
            for y in range(own.shape[2]):

                def tile(t, carry, f=f, y=y, first=first, weights=weights):
                    at = pl.ds(pl.multiple_of(t * 8, 8), 8)
                    values = [
                        ref[j, f, y, at, :] for ref in (own, r1, r2, r3) for j in range(vectors)
                    ]
                    for i in range(2):
                        parts = [w * value for w, value in zip(weights[i], values)]
                        while len(parts) > 1:
                            parts = [a + b for a, b in zip(parts[::2], parts[1::2])]
                        basis[first + i, f, y, at, :] = parts[0]
                    return carry

                lax.fori_loop(0, own.shape[3] // 8, tile, 0, unroll=4)


def shift(value, axis, step):
    count = lax.axis_size(axis)
    return lax.ppermute(value, axis, [(i, (i + step) % count) for i in range(count)])


def swap(value, axis, mask):
    return lax.ppermute(value, axis, [(i, i ^ mask) for i in range(lax.axis_size(axis))])


def summed(value):
    value = (value + swap(value, "vec", 1)) + (swap(value, "vec", 2) + swap(value, "vec", 3))
    mask = 1
    while mask < lax.axis_size("space"):
        value = value + swap(value, "space", mask)
        mask *= 2
    return value


def on_device(tangents, background):
    vectors, fields, rows, columns, levels = tangents.shape
    count = vectors * lax.axis_size("vec")
    cells = fields * rows * columns * levels * lax.axis_size("space")
    me = lax.axis_index("vec").astype(jnp.int32).reshape(1)

    narrow = tangents.astype(jnp.bfloat16)
    bg = jnp.swapaxes(background, 1, 2)
    bg_up = shift(jnp.concatenate([bg[0], bg[1, 1:]]), "space", 1)
    bg_dn = shift(jnp.concatenate([bg[0], bg[1, :1]]), "space", -1)
    up1 = shift(narrow, "space", 1)
    dn1 = shift(narrow, "space", -1)
    up2 = shift(narrow[:, :, 1], "space", 2)
    dn2 = shift(narrow[:, :, 0], "space", -2)
    bg0 = jnp.concatenate([bg_up[:2], bg[0], bg_dn[:2], bg_up[2:], bg[1], bg_dn[2:], bg[2]])
    bg2 = swap(bg0, "vec", 2)
    bg13 = swap(jnp.stack([bg0, bg2]), "vec", 1)

    quarter = jax.ShapeDtypeStruct((vectors, columns, levels), jnp.bfloat16)
    fields_all = 2 * vectors
    adv, q0, q1, q2, q3 = pl.pallas_call(
        advance_kernel,
        out_shape=[jax.ShapeDtypeStruct(tangents.shape, jnp.float32)] + [quarter] * 4,
        in_specs=[SM] + [VM] * 8,
        out_specs=[VM] * 5,
        scratch_shapes=[
            pltpu.VMEM((8, fields_all, columns + 2 * PAD, levels), jnp.float32),
            pltpu.VMEM((6, fields_all, columns + 2 * PAD, levels), jnp.float32),
            pltpu.VMEM((4, fields_all, columns + 2 * PAD, levels), jnp.float32),
            pltpu.VMEM((12, 4, 4, columns // 4, levels), jnp.bfloat16),
        ],
        compiler_params=PARAMS,
        name="advance",
    )(me, tangents, up1, dn1, up2, dn2, bg0, bg2, bg13)

    q1, q2, q3 = swap(q1, "vec", 1), swap(q2, "vec", 2), swap(q3, "vec", 3)
    r2 = lax.ppermute(adv, "vec", [(0, 2), (1, 3)])
    r1 = lax.ppermute(adv, "vec", [(0, 1), (2, 3)])
    r3 = lax.ppermute(r2, "vec", [(2, 3), (3, 2)])

    gram = pl.pallas_call(
        gram_kernel,
        out_shape=jax.ShapeDtypeStruct((count, count), jnp.float32),
        in_specs=[SM] + [VM] * 4,
        out_specs=VM,
        scratch_shapes=[pltpu.VMEM((count, columns, levels), jnp.float32)],
        compiler_params=PARAMS,
        name="gram",
    )(me, q0, q1, q2, q3)
    gram = summed(gram)

    basis, growth = pl.pallas_call(
        functools.partial(final_kernel, 1.0 / cells),
        out_shape=[
            jax.ShapeDtypeStruct(tangents.shape, jnp.float32),
            jax.ShapeDtypeStruct((1, count), jnp.float32),
        ],
        in_specs=[SM] + [VM] * 5,
        out_specs=[VM, VM],
        scratch_shapes=[pltpu.VMEM((count, 2 * count), jnp.float32)],
        compiler_params=PARAMS,
        name="final",
    )(me, gram, adv, r1, r2, r3)
    return basis, growth.reshape(count)


def solution(mesh):
    in_specs = (P("vec", None, "space", None, None), P(None, None, "space", "vec", None))
    out_specs = (P("vec", None, "space", None, None), P())
    return jax.shard_map(
        on_device, mesh=mesh, in_specs=in_specs, out_specs=out_specs, check_vma=False
    )
```

```python
import functools

import jax
import jax.numpy as jnp
from jax import lax
from jax.experimental import pallas as pl
from jax.experimental.pallas import tpu as pltpu
from jax.sharding import PartitionSpec as P

time_step = 0.1
diffusion = 0.5
VM = pl.BlockSpec(memory_space=pltpu.VMEM)
SM = pl.BlockSpec(memory_space=pltpu.SMEM)
PARAMS = pltpu.CompilerParams(vmem_limit_bytes=40 * 1024 * 1024)
PAD = 8
CHUNK = 16


def stage_rows(src, first, bgs, bg_first, alpha, beta, keep, keep_first, rows, vectors, store):
    columns = src.shape[2] - 2 * PAD
    levels = src.shape[3]
    h = beta * time_step
    lane = lax.broadcasted_iota(jnp.int32, (CHUNK, levels), 1)

    def one_row(row, carry):
        at = row + first
        for x in range(0, columns, CHUNK):
            quarter, inner = divmod(x, bgs.shape[3])
            u, v, r, s = (
                bgs[bg_first + row, f, quarter, inner : inner + CHUNK, :].astype(jnp.float32)
                for f in range(4)
            )
            hu, hv, hr, hs = (0.5 * h) * u, (0.5 * h) * v, (0.5 * h) * r, h * s
            lap = diffusion * h
            xn_c, xp_c = lap - hu, lap + hu
            yn_c, yp_c = lap - hv, lap + hv
            zn_c = jnp.where(lane == levels - 1, 0.0, lap - hr)
            zp_c = jnp.where(lane == 0, 0.0, lap + hr)
            mid = beta - 6.0 * lap
            lo = PAD + x
            for vector in range(vectors):
                centers = [src[at, 2 * vector + f, lo : lo + CHUNK, :] for f in range(2)]
                for f in range(2):
                    k = 2 * vector + f
                    c = centers[f]
                    total = xn_c * src[at, k, lo + 1 : lo + 1 + CHUNK, :]
                    total += xp_c * src[at, k, lo - 1 : lo - 1 + CHUNK, :]
                    total += yn_c * src[at + 1, k, lo : lo + CHUNK, :]
                    total += yp_c * src[at - 1, k, lo : lo + CHUNK, :]
                    total += zn_c * pltpu.roll(c, levels - 1, 1)
                    total += zp_c * pltpu.roll(c, 1, 1)
                    total += mid * c
                    if f == 0:
                        total += h * centers[1]
                    else:
                        total -= hs * centers[0]
                    if alpha:
                        total += alpha * keep[row + keep_first, k, lo : lo + CHUNK, :]
                    store(row, vector, f, x, total)
        return carry

    lax.fori_loop(0, rows, one_row, 0)


def wrap(ref, columns):
    ref[:, :, PAD - 1 : PAD, :] = ref[:, :, PAD + columns - 1 : PAD + columns, :]
    ref[:, :, PAD + columns : PAD + columns + 1, :] = ref[:, :, PAD : PAD + 1, :]


def prep_kernel(own, narrow, last, lead):
    vectors, _, rows = own.shape[:3]
    for vector in range(vectors):
        for f in range(2):
            for row in range(rows):
                value = own[vector, f, row].astype(jnp.bfloat16)
                narrow[row, vector, f] = value
                if row == rows - 1:
                    last[vector, f] = value
                if row == 0:
                    lead[vector, f] = value


def advance_kernel(me, own, up1, dn1, up2, dn2, bg0, bg1, bg2, bg3, adv, q0, q1, q2, q3, p0, p1, p2, bgs):
    vectors, _, rows, columns, _ = own.shape
    position = me[0]
    bgs[:, :, position] = bg0[...]
    bgs[:, :, position ^ 2] = bg2[...]
    bgs[:, :, position ^ 1] = bg1[...]
    bgs[:, :, position ^ 3] = bg3[...]
    for vector in range(vectors):
        for f in range(2):
            k = 2 * vector + f
            cells = slice(PAD, PAD + columns)
            p0[0, k, cells, :] = up2[vector, f].astype(jnp.float32)
            p0[7, k, cells, :] = dn2[vector, f].astype(jnp.float32)
            for row in range(2):
                p0[1 + row, k, cells, :] = up1[row, vector, f].astype(jnp.float32)
                p0[3 + row, k, cells, :] = own[vector, f, row]
                p0[5 + row, k, cells, :] = dn1[row, vector, f].astype(jnp.float32)
    wrap(p0, columns)

    def to(ref):
        def store(row, vector, f, x, value):
            ref[row, 2 * vector + f, PAD + x : PAD + x + CHUNK, :] = value

        return store

    def to_out(row, vector, f, x, value):
        adv[vector, f, row, x : x + CHUNK, :] = value

    stage_rows(p0, 1, bgs, 0, 0.0, 1.0, None, 0, 6, vectors, to(p1))
    wrap(p1, columns)
    stage_rows(p1, 1, bgs, 6, 0.75, 0.25, p0, 2, 4, vectors, to(p2))
    wrap(p2, columns)
    stage_rows(p2, 1, bgs, 10, 1.0 / 3.0, 2.0 / 3.0, p0, 3, 2, vectors, to_out)
    for b, q in enumerate((q0, q1, q2, q3)):
        part = position ^ b
        for vector in range(vectors):
            q[vector] = adv[vector, part // 2, part % 2].astype(jnp.bfloat16)


def gram_kernel(me, q0, q1, q2, q3, out, flat):
    vectors, columns, levels = q0.shape
    position = me[0]
    for b, q in enumerate((q0, q1, q2, q3)):
        block = position ^ b
        for vector in range(vectors):
            flat[block * vectors + vector] = q[vector].astype(jnp.float32)
    count = vectors * 4
    rows = flat.reshape(count * columns, levels)
    total = jnp.zeros((count, count), jnp.float32)
    for x in range(0, columns, 2):
        part = jnp.concatenate(
            [rows[pl.ds(x + i, count, stride=columns), :].astype(jnp.bfloat16) for i in range(2)], 1
        )
        total += lax.dot_general(
            part, part, (((1,), (1,)), ((), ())), preferred_element_type=jnp.float32
        )
    out[...] = total


def final_kernel(scale, me, gram, own, r1, r2, r3, basis, growth, inv):
    vectors = own.shape[0]
    count = gram.shape[0]
    position = me[0]
    row = lax.broadcasted_iota(jnp.int32, (count, 2 * count), 0)
    lane = lax.broadcasted_iota(jnp.int32, (count, 2 * count), 1)
    unit = lane - count
    column = ((unit // vectors) ^ position) * vectors + unit % vectors
    eye = jnp.where((lane >= count) & (row == column), 1.0, 0.0)
    table = jnp.concatenate([gram[...] * scale, jnp.zeros((count, count), jnp.float32)], 1) + eye
    pivots = jnp.zeros((1, count), jnp.float32)
    wide = lax.broadcasted_iota(jnp.int32, (1, count), 1)
    for k in range(count):
        pivot = table[k : k + 1, k : k + 1]
        pivots = jnp.where(wide == k, pivot, pivots)
        scaled = table[k : k + 1, :] / jnp.sqrt(pivot)
        below = jnp.where(row[:, :1] > k, table[:, k : k + 1] / jnp.sqrt(pivot), 0.0)
        table = jnp.where(row == k, scaled, table - below * scaled)
    growth[...] = 0.5 * jnp.log(pivots)
    inv[...] = table
    for first in range(0, vectors, 2):
        weights = []
        for i in range(first, first + 2):
            line = inv[pl.ds(position * vectors + i, 1), :]
            weights.append(
                [
                    jnp.broadcast_to(line[:, count + j : count + j + 1], (8, own.shape[4]))
                    for j in range(count)
                ]
            )
        for f in range(own.shape[1]):
            for y in range(own.shape[2]):

                def tile(t, carry, f=f, y=y, first=first, weights=weights):
                    at = pl.ds(pl.multiple_of(t * 8, 8), 8)
                    values = [
                        ref[j, f, y, at, :] for ref in (own, r1, r2, r3) for j in range(vectors)
                    ]
                    for i in range(2):
                        parts = [w * value for w, value in zip(weights[i], values)]
                        while len(parts) > 1:
                            parts = [a + b for a, b in zip(parts[::2], parts[1::2])]
                        basis[first + i, f, y, at, :] = parts[0]
                    return carry

                lax.fori_loop(0, own.shape[3] // 8, tile, 0, unroll=4)


def shift(value, axis, step):
    count = lax.axis_size(axis)
    return lax.ppermute(value, axis, [(i, (i + step) % count) for i in range(count)])


def swap(value, axis, mask):
    return lax.ppermute(value, axis, [(i, i ^ mask) for i in range(lax.axis_size(axis))])


def summed(value):
    value = (value + swap(value, "vec", 1)) + (swap(value, "vec", 2) + swap(value, "vec", 3))
    mask = 1
    while mask < lax.axis_size("space"):
        value = value + swap(value, "space", mask)
        mask *= 2
    return value


def on_device(tangents, background):
    vectors, fields, rows, columns, levels = tangents.shape
    count = vectors * lax.axis_size("vec")
    cells = fields * rows * columns * levels * lax.axis_size("space")
    me = lax.axis_index("vec").astype(jnp.int32).reshape(1)

    row_shape = jax.ShapeDtypeStruct((vectors, fields, columns, levels), jnp.bfloat16)
    narrow, last, lead = pl.pallas_call(
        prep_kernel,
        out_shape=[jax.ShapeDtypeStruct((rows,) + row_shape.shape, jnp.bfloat16), row_shape, row_shape],
        in_specs=[VM],
        out_specs=[VM] * 3,
        compiler_params=PARAMS,
        name="prep",
    )(tangents)
    bg = jnp.swapaxes(background, 1, 2)
    bg_up = shift(jnp.concatenate([bg[0], bg[1, 1:]]), "space", 1)
    bg_dn = shift(jnp.concatenate([bg[0], bg[1, :1]]), "space", -1)
    up1 = shift(narrow, "space", 1)
    dn1 = shift(narrow, "space", -1)
    up2 = shift(last, "space", 2)
    dn2 = shift(lead, "space", -2)
    bg0 = jnp.concatenate([bg_up[:2], bg[0], bg_dn[:2], bg_up[2:], bg[1], bg_dn[2:], bg[2]])
    bg1, bg2, bg3 = (swap(bg0, "vec", mask) for mask in (1, 2, 3))

    quarter = jax.ShapeDtypeStruct((vectors, columns, levels), jnp.bfloat16)
    fields_all = 2 * vectors
    adv, q0, q1, q2, q3 = pl.pallas_call(
        advance_kernel,
        out_shape=[jax.ShapeDtypeStruct(tangents.shape, jnp.float32)] + [quarter] * 4,
        in_specs=[SM] + [VM] * 9,
        out_specs=[VM] * 5,
        scratch_shapes=[
            pltpu.VMEM((8, fields_all, columns + 2 * PAD, levels), jnp.float32),
            pltpu.VMEM((6, fields_all, columns + 2 * PAD, levels), jnp.float32),
            pltpu.VMEM((4, fields_all, columns + 2 * PAD, levels), jnp.float32),
            pltpu.VMEM((12, 4, 4, columns // 4, levels), jnp.bfloat16),
        ],
        compiler_params=PARAMS,
        name="advance",
    )(me, tangents, up1, dn1, up2, dn2, bg0, bg1, bg2, bg3)

    q1, q2, q3 = swap(q1, "vec", 1), swap(q2, "vec", 2), swap(q3, "vec", 3)
    r2 = lax.ppermute(adv, "vec", [(0, 2), (1, 3)])
    r1 = lax.ppermute(adv, "vec", [(0, 1), (2, 3)])
    gram = pl.pallas_call(
        gram_kernel,
        out_shape=jax.ShapeDtypeStruct((count, count), jnp.float32),
        in_specs=[SM] + [VM] * 4,
        out_specs=VM,
        scratch_shapes=[pltpu.VMEM((count, columns, levels), jnp.float32)],
        compiler_params=PARAMS,
        name="gram",
    )(me, q0, q1, q2, q3)
    gram = summed(gram)
    gram, r2 = lax.optimization_barrier((gram, r2))
    r3 = lax.ppermute(r2, "vec", [(2, 3), (3, 2)])

    basis, growth = pl.pallas_call(
        functools.partial(final_kernel, 1.0 / cells),
        out_shape=[
            jax.ShapeDtypeStruct(tangents.shape, jnp.float32),
            jax.ShapeDtypeStruct((1, count), jnp.float32),
        ],
        in_specs=[SM] + [VM] * 5,
        out_specs=[VM, VM],
        scratch_shapes=[pltpu.VMEM((count, 2 * count), jnp.float32)],
        compiler_params=PARAMS,
        name="final",
    )(me, gram, adv, r1, r2, r3)
    return basis, growth.reshape(count)


def solution(mesh):
    in_specs = (P("vec", None, "space", None, None), P(None, None, "space", "vec", None))
    out_specs = (P("vec", None, "space", None, None), P())
    return jax.shard_map(
        on_device, mesh=mesh, in_specs=in_specs, out_specs=out_specs, check_vma=False
    )
```

```python
import functools

import jax
import jax.numpy as jnp
from jax import lax
from jax.experimental import pallas as pl
from jax.experimental.pallas import tpu as pltpu
from jax.sharding import PartitionSpec as P

time_step = 0.1
diffusion = 0.5
VM = pl.BlockSpec(memory_space=pltpu.VMEM)
SM = pl.BlockSpec(memory_space=pltpu.SMEM)
PARAMS = pltpu.CompilerParams(vmem_limit_bytes=40 * 1024 * 1024)
PAD = 8
CHUNK = 16


def stage_rows(src, first, bgs, bg_first, alpha, beta, keep, keep_first, rows, vectors, store):
    columns = src.shape[2] - 2 * PAD
    levels = src.shape[3]
    h = beta * time_step
    lane = lax.broadcasted_iota(jnp.int32, (CHUNK, levels), 1)

    def one_row(row, carry):
        at = row + first
        for x in range(0, columns, CHUNK):
            quarter, inner = divmod(x, bgs.shape[3])
            u, v, r, s = (
                bgs[bg_first + row, f, quarter, inner : inner + CHUNK, :].astype(jnp.float32)
                for f in range(4)
            )
            hu, hv, hr, hs = (0.5 * h) * u, (0.5 * h) * v, (0.5 * h) * r, h * s
            lap = diffusion * h
            xn_c, xp_c = lap - hu, lap + hu
            yn_c, yp_c = lap - hv, lap + hv
            zn_c = jnp.where(lane == levels - 1, 0.0, lap - hr)
            zp_c = jnp.where(lane == 0, 0.0, lap + hr)
            mid = beta - 6.0 * lap
            lo = PAD + x
            for vector in range(vectors):
                centers = [src[at, 2 * vector + f, lo : lo + CHUNK, :] for f in range(2)]
                for f in range(2):
                    k = 2 * vector + f
                    c = centers[f]
                    total = xn_c * src[at, k, lo + 1 : lo + 1 + CHUNK, :]
                    total += xp_c * src[at, k, lo - 1 : lo - 1 + CHUNK, :]
                    total += yn_c * src[at + 1, k, lo : lo + CHUNK, :]
                    total += yp_c * src[at - 1, k, lo : lo + CHUNK, :]
                    total += zn_c * pltpu.roll(c, levels - 1, 1)
                    total += zp_c * pltpu.roll(c, 1, 1)
                    total += mid * c
                    if f == 0:
                        total += h * centers[1]
                    else:
                        total -= hs * centers[0]
                    if alpha:
                        total += alpha * keep[row + keep_first, k, lo : lo + CHUNK, :]
                    store(row, vector, f, x, total)
        return carry

    lax.fori_loop(0, rows, one_row, 0)


def wrap(ref, columns):
    ref[:, :, PAD - 1 : PAD, :] = ref[:, :, PAD + columns - 1 : PAD + columns, :]
    ref[:, :, PAD + columns : PAD + columns + 1, :] = ref[:, :, PAD : PAD + 1, :]


def prep_kernel(own, narrow, last, lead):
    vectors, _, rows = own.shape[:3]
    for vector in range(vectors):
        for f in range(2):
            for row in range(rows):
                value = own[vector, f, row].astype(jnp.bfloat16)
                narrow[row, vector, f] = value
                if row == rows - 1:
                    last[vector, f] = value
                if row == 0:
                    lead[vector, f] = value


def edges_kernel(background, up, dn):
    for f in range(4):
        for row in range(2):
            up[row, f] = background[0, f, row]
            dn[row, f] = background[0, f, row]
        up[2, f] = background[1, f, 1]
        dn[2, f] = background[1, f, 0]


def pack_kernel(background, up, dn, packed):
    for f in range(4):
        for row in range(2):
            packed[row, f] = up[row, f]
            packed[2 + row, f] = background[0, f, row]
            packed[4 + row, f] = dn[row, f]
            packed[7 + row, f] = background[1, f, row]
            packed[10 + row, f] = background[2, f, row]
        packed[6, f] = up[2, f]
        packed[9, f] = dn[2, f]


def advance_kernel(me, own, up1, dn1, up2, dn2, bg0, bg1, bg2, bg3, adv, hi, lo, p0, p1, p2, bgs):
    vectors, _, rows, columns, _ = own.shape
    position = me[0]
    bgs[:, :, position] = bg0[...]
    bgs[:, :, position ^ 2] = bg2[...]
    bgs[:, :, position ^ 1] = bg1[...]
    bgs[:, :, position ^ 3] = bg3[...]
    for vector in range(vectors):
        for f in range(2):
            k = 2 * vector + f
            cells = slice(PAD, PAD + columns)
            p0[0, k, cells, :] = up2[vector, f].astype(jnp.float32)
            p0[7, k, cells, :] = dn2[vector, f].astype(jnp.float32)
            for row in range(2):
                p0[1 + row, k, cells, :] = up1[row, vector, f].astype(jnp.float32)
                p0[3 + row, k, cells, :] = own[vector, f, row]
                p0[5 + row, k, cells, :] = dn1[row, vector, f].astype(jnp.float32)
    wrap(p0, columns)

    def to(ref):
        def store(row, vector, f, x, value):
            ref[row, 2 * vector + f, PAD + x : PAD + x + CHUNK, :] = value

        return store

    def to_out(row, vector, f, x, value):
        adv[vector, f, row, x : x + CHUNK, :] = value
        top = value.astype(jnp.bfloat16)
        hi[vector, f, row, x : x + CHUNK, :] = top
        lo[vector, f, row, x : x + CHUNK, :] = (value - top.astype(jnp.float32)).astype(jnp.bfloat16)

    stage_rows(p0, 1, bgs, 0, 0.0, 1.0, None, 0, 6, vectors, to(p1))
    wrap(p1, columns)
    stage_rows(p1, 1, bgs, 6, 0.75, 0.25, p0, 2, 4, vectors, to(p2))
    wrap(p2, columns)
    stage_rows(p2, 1, bgs, 10, 1.0 / 3.0, 2.0 / 3.0, p0, 3, 2, vectors, to_out)


def gram_kernel(me, h0, h1, h2, h3, out, lines):
    vectors, fields, rows, columns, levels = h0.shape
    count = 4 * vectors
    size = count * CHUNK
    position = me[0]
    parts = []
    for f in range(fields):
        for y in range(rows):
            for x in range(0, columns, CHUNK):
                parts.append(
                    jnp.concatenate(
                        [h[j, f, y, x : x + CHUNK, :] for h in (h0, h1, h2, h3) for j in range(vectors)]
                    )
                )
    flat = jnp.concatenate(parts, 1)
    full = lax.dot_general(flat, flat, (((1,), (1,)), ((), ())), preferred_element_type=jnp.float32)
    row = lax.broadcasted_iota(jnp.int32, (size, size), 0)
    lane = lax.broadcasted_iota(jnp.int32, (size, size), 1)
    full = jnp.where(row % CHUNK == lane % CHUNK, full, 0.0)
    full = jnp.sum(full.reshape(count, CHUNK, size), axis=1)
    for b in range(4):
        for j in range(vectors):
            k = b * vectors + j
            lines[pl.ds((position ^ b) * vectors + j, 1), :] = full[k : k + 1, :]
    group = lax.broadcasted_iota(jnp.int32, (size, count), 0) // CHUNK
    target = ((group // vectors) ^ position) * vectors + group % vectors
    pick = jnp.where(target == lax.broadcasted_iota(jnp.int32, (size, count), 1), 1.0, 0.0)
    out[...] = jnp.dot(
        lines[...], pick, precision=lax.Precision.HIGHEST, preferred_element_type=jnp.float32
    )


def final_kernel(scale, me, gram, own, h1, h2, h3, l1, l2, l3, basis, growth, inv):
    vectors = own.shape[0]
    count = gram.shape[0]
    position = me[0]
    row = lax.broadcasted_iota(jnp.int32, (count, 2 * count), 0)
    lane = lax.broadcasted_iota(jnp.int32, (count, 2 * count), 1)
    unit = lane - count
    column = ((unit // vectors) ^ position) * vectors + unit % vectors
    eye = jnp.where((lane >= count) & (row == column), 1.0, 0.0)
    table = jnp.concatenate([gram[...] * scale, jnp.zeros((count, count), jnp.float32)], 1) + eye
    pivots = jnp.zeros((1, count), jnp.float32)
    wide = lax.broadcasted_iota(jnp.int32, (1, count), 1)
    for k in range(count):
        pivot = table[k : k + 1, k : k + 1]
        pivots = jnp.where(wide == k, pivot, pivots)
        scaled = table[k : k + 1, :] / jnp.sqrt(pivot)
        below = jnp.where(row[:, :1] > k, table[:, k : k + 1] / jnp.sqrt(pivot), 0.0)
        table = jnp.where(row == k, scaled, table - below * scaled)
    growth[...] = 0.5 * jnp.log(pivots)
    inv[...] = table
    for first in range(0, vectors, 2):
        weights = []
        for i in range(first, first + 2):
            line = inv[pl.ds(position * vectors + i, 1), :]
            weights.append(
                [
                    jnp.broadcast_to(line[:, count + j : count + j + 1], (CHUNK, own.shape[4]))
                    for j in range(count)
                ]
            )
        for f in range(own.shape[1]):
            for y in range(own.shape[2]):

                def tile(t, carry, f=f, y=y, first=first, weights=weights):
                    at = pl.ds(pl.multiple_of(t * CHUNK, CHUNK), CHUNK)
                    values = [own[j, f, y, at, :] for j in range(vectors)]
                    for h, l in ((h1, l1), (h2, l2), (h3, l3)):
                        for j in range(vectors):
                            values.append(
                                h[j, f, y, at, :].astype(jnp.float32)
                                + l[j, f, y, at, :].astype(jnp.float32)
                            )
                    for i in range(2):
                        parts = [w * value for w, value in zip(weights[i], values)]
                        while len(parts) > 1:
                            parts = [a + b for a, b in zip(parts[::2], parts[1::2])]
                        basis[first + i, f, y, at, :] = parts[0]
                    return carry

                lax.fori_loop(0, own.shape[3] // CHUNK, tile, 0, unroll=2)


def shift(value, axis, step):
    count = lax.axis_size(axis)
    return lax.ppermute(value, axis, [(i, (i + step) % count) for i in range(count)])


def swap(value, axis, mask):
    return lax.ppermute(value, axis, [(i, i ^ mask) for i in range(lax.axis_size(axis))])


def summed(value):
    mask, size = 2, lax.axis_size("space")
    while mask < size:
        if 2 * mask < size:
            one, two, three = (swap(value, "space", k) for k in (mask, 2 * mask, 3 * mask))
            value = (value + one) + (two + three)
        else:
            value = value + swap(value, "space", mask)
        mask *= 4
    return value


def on_device(tangents, background):
    vectors, fields, rows, columns, levels = tangents.shape
    count = vectors * lax.axis_size("vec")
    cells = fields * rows * columns * levels * lax.axis_size("space")
    me = lax.axis_index("vec").astype(jnp.int32).reshape(1)

    row_shape = jax.ShapeDtypeStruct((vectors, fields, columns, levels), jnp.bfloat16)
    narrow, last, lead = pl.pallas_call(
        prep_kernel,
        out_shape=[jax.ShapeDtypeStruct((rows,) + row_shape.shape, jnp.bfloat16), row_shape, row_shape],
        in_specs=[VM],
        out_specs=[VM] * 3,
        compiler_params=PARAMS,
        name="prep",
    )(tangents)
    edge = jax.ShapeDtypeStruct((3, 4) + background.shape[3:], jnp.bfloat16)
    bg_up, bg_dn = pl.pallas_call(
        edges_kernel,
        out_shape=[edge, edge],
        in_specs=[VM],
        out_specs=[VM] * 2,
        compiler_params=PARAMS,
        name="edges",
    )(background)
    bg_up = shift(bg_up, "space", 1)
    bg_dn = shift(bg_dn, "space", -1)
    narrow, last, lead, bg_up, bg_dn = lax.optimization_barrier((narrow, last, lead, bg_up, bg_dn))
    up1 = shift(narrow, "space", 1)
    dn1 = shift(narrow, "space", -1)
    up2 = shift(last, "space", 2)
    dn2 = shift(lead, "space", -2)
    bg0 = pl.pallas_call(
        pack_kernel,
        out_shape=jax.ShapeDtypeStruct((12, 4) + background.shape[3:], jnp.bfloat16),
        in_specs=[VM] * 3,
        out_specs=VM,
        compiler_params=PARAMS,
        name="pack",
    )(background, bg_up, bg_dn)
    bg1, bg2, bg3 = (swap(bg0, "vec", mask) for mask in (1, 2, 3))

    half = jax.ShapeDtypeStruct(tangents.shape, jnp.bfloat16)
    fields_all = 2 * vectors
    adv, hi, lo = pl.pallas_call(
        advance_kernel,
        out_shape=[jax.ShapeDtypeStruct(tangents.shape, jnp.float32), half, half],
        in_specs=[SM] + [VM] * 9,
        out_specs=[VM] * 3,
        scratch_shapes=[
            pltpu.VMEM((8, fields_all, columns + 2 * PAD, levels), jnp.float32),
            pltpu.VMEM((6, fields_all, columns + 2 * PAD, levels), jnp.float32),
            pltpu.VMEM((4, fields_all, columns + 2 * PAD, levels), jnp.float32),
            pltpu.VMEM((12, 4, 4, columns // 4, levels), jnp.bfloat16),
        ],
        compiler_params=PARAMS,
        name="advance",
    )(me, tangents, up1, dn1, up2, dn2, bg0, bg1, bg2, bg3)

    h2, h1 = swap(hi, "vec", 2), swap(hi, "vec", 1)
    l2, l1 = swap(lo, "vec", 2), swap(lo, "vec", 1)
    h3 = swap(h2, "vec", 1)

    gram = pl.pallas_call(
        gram_kernel,
        out_shape=jax.ShapeDtypeStruct((count, count), jnp.float32),
        in_specs=[SM] + [VM] * 4,
        out_specs=VM,
        scratch_shapes=[pltpu.VMEM((count, count * CHUNK), jnp.float32)],
        compiler_params=PARAMS,
        name="gram",
    )(me, hi, h1, h2, h3)
    gram = gram + swap(gram, "space", 1)
    gram, l2 = lax.optimization_barrier((gram, l2))
    l3 = swap(l2, "vec", 1)
    gram = summed(gram)

    basis, growth = pl.pallas_call(
        functools.partial(final_kernel, 1.0 / cells),
        out_shape=[
            jax.ShapeDtypeStruct(tangents.shape, jnp.float32),
            jax.ShapeDtypeStruct((1, count), jnp.float32),
        ],
        in_specs=[SM] + [VM] * 8,
        out_specs=[VM, VM],
        scratch_shapes=[pltpu.VMEM((count, 2 * count), jnp.float32)],
        compiler_params=PARAMS,
        name="final",
    )(me, gram, adv, h1, h2, h3, l1, l2, l3)
    return basis, growth.reshape(count)


def solution(mesh):
    in_specs = (P("vec", None, "space", None, None), P(None, None, "space", "vec", None))
    out_specs = (P("vec", None, "space", None, None), P())
    return jax.shard_map(
        on_device, mesh=mesh, in_specs=in_specs, out_specs=out_specs, check_vma=False
    )
```

```python
import functools

import jax
import jax.numpy as jnp
from jax import lax
from jax.experimental import pallas as pl
from jax.experimental.pallas import tpu as pltpu
from jax.sharding import PartitionSpec as P

time_step = 0.1
diffusion = 0.5
VM = pl.BlockSpec(memory_space=pltpu.VMEM)
SM = pl.BlockSpec(memory_space=pltpu.SMEM)
SMALL = pltpu.CompilerParams(vmem_limit_bytes=12 * 1024 * 1024)
PARAMS = pltpu.CompilerParams(vmem_limit_bytes=20 * 1024 * 1024)
PAD = 8
CHUNK = 16


def stage_rows(src, first, bgs, bg_first, alpha, beta, keep, keep_first, rows, vectors, store):
    columns = src.shape[2] - 2 * PAD
    levels = src.shape[3]
    h = beta * time_step
    lane = lax.broadcasted_iota(jnp.int32, (CHUNK, levels), 1)

    def one_row(row, carry):
        at = row + first
        for x in range(0, columns, CHUNK):
            quarter, inner = divmod(x, bgs.shape[3])
            u, v, r, s = (
                bgs[quarter, bg_first + row, f, inner : inner + CHUNK, :].astype(jnp.float32)
                for f in range(4)
            )
            hu, hv, hr, hs = (0.5 * h) * u, (0.5 * h) * v, (0.5 * h) * r, h * s
            lap = diffusion * h
            xn_c, xp_c = lap - hu, lap + hu
            yn_c, yp_c = lap - hv, lap + hv
            zn_c = jnp.where(lane == levels - 1, 0.0, lap - hr)
            zp_c = jnp.where(lane == 0, 0.0, lap + hr)
            mid = beta - 6.0 * lap
            lo = PAD + x
            for vector in range(vectors):
                centers = [src[at, 2 * vector + f, lo : lo + CHUNK, :] for f in range(2)]
                for f in range(2):
                    k = 2 * vector + f
                    c = centers[f]
                    total = xn_c * src[at, k, lo + 1 : lo + 1 + CHUNK, :]
                    total += xp_c * src[at, k, lo - 1 : lo - 1 + CHUNK, :]
                    total += yn_c * src[at + 1, k, lo : lo + CHUNK, :]
                    total += yp_c * src[at - 1, k, lo : lo + CHUNK, :]
                    total += zn_c * pltpu.roll(c, levels - 1, 1)
                    total += zp_c * pltpu.roll(c, 1, 1)
                    total += mid * c
                    if f == 0:
                        total += h * centers[1]
                    else:
                        total -= hs * centers[0]
                    if alpha:
                        total += alpha * keep[row + keep_first, k, lo : lo + CHUNK, :]
                    store(row, vector, f, x, total)
        return carry

    lax.fori_loop(0, rows, one_row, 0)


def wrap(ref, columns):
    ref[:, :, PAD - 1 : PAD, :] = ref[:, :, PAD + columns - 1 : PAD + columns, :]
    ref[:, :, PAD + columns : PAD + columns + 1, :] = ref[:, :, PAD : PAD + 1, :]


def prep_kernel(own, narrow, last, lead):
    vectors, _, rows = own.shape[:3]
    for vector in range(vectors):
        for f in range(2):
            for row in range(rows):
                value = own[vector, f, row].astype(jnp.bfloat16)
                narrow[row, vector, f] = value
                if row == rows - 1:
                    last[vector, f] = value
                if row == 0:
                    lead[vector, f] = value


def edges_kernel(background, up, dn):
    for f in range(4):
        for row in range(2):
            up[row, f] = background[0, f, row]
            dn[row, f] = background[0, f, row]
        up[2, f] = background[1, f, 1]
        dn[2, f] = background[1, f, 0]


def pack_kernel(background, up, dn, packed):
    for f in range(4):
        for row in range(2):
            packed[row, f] = up[row, f]
            packed[2 + row, f] = background[0, f, row]
            packed[4 + row, f] = dn[row, f]
            packed[7 + row, f] = background[1, f, row]
            packed[10 + row, f] = background[2, f, row]
        packed[6, f] = up[2, f]
        packed[9, f] = dn[2, f]


def advance_kernel(me, own, up1, dn1, up2, dn2, bg0, bg1, bg2, bg3, adv, hia, hib, lo, p0, p1, p2, bg):
    vectors, _, rows, columns, _ = own.shape
    for mask, part in enumerate((bg0, bg1, bg2, bg3)):
        bg[me[0] ^ mask] = part[...]
    for vector in range(vectors):
        for f in range(2):
            k = 2 * vector + f
            cells = slice(PAD, PAD + columns)
            p0[0, k, cells, :] = up2[vector, f].astype(jnp.float32)
            p0[7, k, cells, :] = dn2[vector, f].astype(jnp.float32)
            for row in range(2):
                p0[1 + row, k, cells, :] = up1[row, vector, f].astype(jnp.float32)
                p0[3 + row, k, cells, :] = own[vector, f, row]
                p0[5 + row, k, cells, :] = dn1[row, vector, f].astype(jnp.float32)
    wrap(p0, columns)

    def to(ref):
        def store(row, vector, f, x, value):
            ref[row, 2 * vector + f, PAD + x : PAD + x + CHUNK, :] = value

        return store

    def to_out(row, vector, f, x, value):
        adv[vector, f, row, x : x + CHUNK, :] = value
        top = value.astype(jnp.bfloat16)
        hi = (hia, hib)[vector // 2]
        hi[vector % 2, f, row, x : x + CHUNK, :] = top
        lo[vector, f, row, x : x + CHUNK, :] = (value - top.astype(jnp.float32)).astype(jnp.bfloat16)

    stage_rows(p0, 1, bg, 0, 0.0, 1.0, None, 0, 6, vectors, to(p1))
    wrap(p1, columns)
    stage_rows(p1, 1, bg, 6, 0.75, 0.25, p0, 2, 4, vectors, to(p2))
    wrap(p2, columns)
    stage_rows(p2, 1, bg, 10, 1.0 / 3.0, 2.0 / 3.0, p0, 3, 2, vectors, to_out)


def stacked(blocks):
    vectors, fields, rows, columns, _ = blocks[0].shape
    parts = []
    for f in range(fields):
        for y in range(rows):
            for x in range(0, columns, CHUNK):
                parts.append(
                    jnp.concatenate(
                        [h[j, f, y, x : x + CHUNK, :] for h in blocks for j in range(vectors)]
                    )
                )
    return jnp.concatenate(parts, 1)


def pairs(left, right):
    full = lax.dot_general(left, right, (((1,), (1,)), ((), ())), preferred_element_type=jnp.float32)
    row = lax.broadcasted_iota(jnp.int32, full.shape, 0)
    lane = lax.broadcasted_iota(jnp.int32, full.shape, 1)
    full = jnp.where(row % CHUNK == lane % CHUNK, full, 0.0)
    return jnp.sum(full.reshape(full.shape[0] // CHUNK, CHUNK, full.shape[1]), axis=1)


def gram_own_kernel(h0a, h0b, h1a, h1b, out):
    flat = stacked((h0a, h0b, h1a, h1b))
    out[...] = pairs(flat, flat)


def gram_kernel(me, near, h0a, h0b, h1a, h1b, h2a, h2b, h3a, h3b, out, lines):
    vectors = 2 * h0a.shape[0]
    count = 4 * vectors
    size = count * CHUNK
    position = me[0]
    flat, other = stacked((h0a, h0b, h1a, h1b)), stacked((h2a, h2b, h3a, h3b))
    cross = pairs(flat, other)
    far = pairs(other, other)
    for b in range(2):
        for j in range(vectors):
            k = b * vectors + j
            lines[pl.ds((position ^ b) * vectors + j, 1), :] = jnp.concatenate(
                [near[k : k + 1, :], cross[k : k + 1, :]], 1
            )
            lines[pl.ds((position ^ (2 + b)) * vectors + j, 1), :] = jnp.concatenate(
                [jnp.zeros_like(far[k : k + 1, :]), far[k : k + 1, :]], 1
            )
    group = lax.broadcasted_iota(jnp.int32, (size, count), 0) // CHUNK
    target = ((group // vectors) ^ position) * vectors + group % vectors
    pick = jnp.where(target == lax.broadcasted_iota(jnp.int32, (size, count), 1), 1.0, 0.0)
    half = jnp.dot(
        lines[...], pick, precision=lax.Precision.HIGHEST, preferred_element_type=jnp.float32
    )
    row = lax.broadcasted_iota(jnp.int32, (count, count), 0) // (2 * vectors)
    lane = lax.broadcasted_iota(jnp.int32, (count, count), 1) // (2 * vectors)
    out[...] = half + jnp.where(row == lane, 0.0, half.T)


def final_kernel(scale, me, gram, own, h1a, h1b, h2a, h2b, h3a, h3b, l1, l2, l3, basis, growth, inv):
    vectors = own.shape[0]
    count = gram.shape[0]
    position = me[0]
    row = lax.broadcasted_iota(jnp.int32, (count, 2 * count), 0)
    lane = lax.broadcasted_iota(jnp.int32, (count, 2 * count), 1)
    unit = lane - count
    column = ((unit // vectors) ^ position) * vectors + unit % vectors
    eye = jnp.where((lane >= count) & (row == column), 1.0, 0.0)
    table = jnp.concatenate([gram[...] * scale, jnp.zeros((count, count), jnp.float32)], 1) + eye
    pivots = jnp.zeros((1, count), jnp.float32)
    wide = lax.broadcasted_iota(jnp.int32, (1, count), 1)
    for k in range(count):
        pivot = table[k : k + 1, k : k + 1]
        pivots = jnp.where(wide == k, pivot, pivots)
        scaled = table[k : k + 1, :] / jnp.sqrt(pivot)
        below = jnp.where(row[:, :1] > k, table[:, k : k + 1] / jnp.sqrt(pivot), 0.0)
        table = jnp.where(row == k, scaled, table - below * scaled)
    growth[...] = 0.5 * jnp.log(pivots)
    inv[...] = table
    for first in range(0, vectors, 2):
        weights = []
        for i in range(first, first + 2):
            line = inv[pl.ds(position * vectors + i, 1), :]
            weights.append(
                [
                    jnp.broadcast_to(line[:, count + j : count + j + 1], (CHUNK, own.shape[4]))
                    for j in range(count)
                ]
            )
        for f in range(own.shape[1]):
            for y in range(own.shape[2]):

                def tile(t, carry, f=f, y=y, first=first, weights=weights):
                    at = pl.ds(pl.multiple_of(t * CHUNK, CHUNK), CHUNK)
                    values = [own[j, f, y, at, :] for j in range(vectors)]
                    for h, l in (((h1a, h1b), l1), ((h2a, h2b), l2), ((h3a, h3b), l3)):
                        for j in range(vectors):
                            values.append(
                                h[j // 2][j % 2, f, y, at, :].astype(jnp.float32)
                                + l[j, f, y, at, :].astype(jnp.float32)
                            )
                    for i in range(2):
                        parts = [w * value for w, value in zip(weights[i], values)]
                        while len(parts) > 1:
                            parts = [a + b for a, b in zip(parts[::2], parts[1::2])]
                        basis[first + i, f, y, at, :] = parts[0]
                    return carry

                lax.fori_loop(0, own.shape[3] // CHUNK, tile, 0, unroll=2)


def shift(value, axis, step):
    count = lax.axis_size(axis)
    return lax.ppermute(value, axis, [(i, (i + step) % count) for i in range(count)])


def swap(value, axis, mask):
    return lax.ppermute(value, axis, [(i, i ^ mask) for i in range(lax.axis_size(axis))])


def summed(value):
    mask, size = 2, lax.axis_size("space")
    while mask < size:
        if 2 * mask < size:
            one, two, three = (swap(value, "space", k) for k in (mask, 2 * mask, 3 * mask))
            value = (value + one) + (two + three)
        else:
            value = value + swap(value, "space", mask)
        mask *= 4
    return value


def on_device(tangents, background):
    vectors, fields, rows, columns, levels = tangents.shape
    count = vectors * lax.axis_size("vec")
    cells = fields * rows * columns * levels * lax.axis_size("space")
    me = lax.axis_index("vec").astype(jnp.int32).reshape(1)

    row_shape = jax.ShapeDtypeStruct((vectors, fields, columns, levels), jnp.bfloat16)
    narrow, last, lead = pl.pallas_call(
        prep_kernel,
        out_shape=[jax.ShapeDtypeStruct((rows,) + row_shape.shape, jnp.bfloat16), row_shape, row_shape],
        in_specs=[VM],
        out_specs=[VM] * 3,
        compiler_params=SMALL,
        name="prep",
    )(tangents)
    edge = jax.ShapeDtypeStruct((3, 4) + background.shape[3:], jnp.bfloat16)
    bg_up, bg_dn = pl.pallas_call(
        edges_kernel,
        out_shape=[edge, edge],
        in_specs=[VM],
        out_specs=[VM] * 2,
        compiler_params=SMALL,
        name="edges",
    )(background)
    bg_up = shift(bg_up, "space", 1)
    bg_dn = shift(bg_dn, "space", -1)
    narrow, last, lead, bg_up, bg_dn = lax.optimization_barrier((narrow, last, lead, bg_up, bg_dn))
    up1 = shift(narrow, "space", 1)
    dn1 = shift(narrow, "space", -1)
    up2 = shift(last, "space", 2)
    dn2 = shift(lead, "space", -2)
    packed = pl.pallas_call(
        pack_kernel,
        out_shape=jax.ShapeDtypeStruct((12, 4) + background.shape[3:], jnp.bfloat16),
        in_specs=[VM] * 3,
        out_specs=VM,
        compiler_params=SMALL,
        name="pack",
    )(background, bg_up, bg_dn)
    bg2 = swap(packed, "vec", 2)
    near_bg, far_bg, up2, dn2 = lax.optimization_barrier((packed, bg2, up2, dn2))
    bgs = [packed, swap(near_bg, "vec", 1), bg2, swap(far_bg, "vec", 1)]

    low = jax.ShapeDtypeStruct(tangents.shape, jnp.bfloat16)
    pair = jax.ShapeDtypeStruct((vectors // 2,) + tangents.shape[1:], jnp.bfloat16)
    fields_all = 2 * vectors
    adv, hia, hib, lo = pl.pallas_call(
        advance_kernel,
        out_shape=[jax.ShapeDtypeStruct(tangents.shape, jnp.float32), pair, pair, low],
        in_specs=[SM] + [VM] * 9,
        out_specs=[VM] * 4,
        scratch_shapes=[
            pltpu.VMEM((8, fields_all, columns + 2 * PAD, levels), jnp.float32),
            pltpu.VMEM((6, fields_all, columns + 2 * PAD, levels), jnp.float32),
            pltpu.VMEM((4, fields_all, columns + 2 * PAD, levels), jnp.float32),
            pltpu.VMEM((4,) + packed.shape, jnp.bfloat16),
            ],
        compiler_params=PARAMS,
        name="advance",
    )(me, tangents, up1, dn1, up2, dn2, *bgs)

    h2a, h1a = swap(hia, "vec", 2), swap(hia, "vec", 1)
    h2b, h1b = swap(hib, "vec", 2), swap(hib, "vec", 1)
    near = pl.pallas_call(
        gram_own_kernel,
        out_shape=jax.ShapeDtypeStruct((2 * vectors, 2 * vectors * CHUNK), jnp.float32),
        in_specs=[VM] * 4,
        out_specs=VM,
        compiler_params=SMALL,
        name="gram_own",
    )(hia, hib, h1a, h1b)
    lo, near = lax.optimization_barrier((lo, near))
    l2, l1 = swap(lo, "vec", 2), swap(lo, "vec", 1)
    h3a, h3b = swap(h2a, "vec", 1), swap(h2b, "vec", 1)
    high = (hia, hib, h1a, h1b, h2a, h2b, h3a, h3b)

    gram = pl.pallas_call(
        gram_kernel,
        out_shape=jax.ShapeDtypeStruct((count, count), jnp.float32),
        in_specs=[SM] + [VM] * 9,
        out_specs=VM,
        scratch_shapes=[pltpu.VMEM((count, count * CHUNK), jnp.float32)],
        compiler_params=SMALL,
        name="gram",
    )(me, near, *high)
    gram = gram + swap(gram, "space", 1)
    gram, l2 = lax.optimization_barrier((gram, l2))
    l3 = swap(l2, "vec", 1)
    gram = summed(gram)

    basis, growth = pl.pallas_call(
        functools.partial(final_kernel, 1.0 / cells),
        out_shape=[
            jax.ShapeDtypeStruct(tangents.shape, jnp.float32),
            jax.ShapeDtypeStruct((1, count), jnp.float32),
        ],
        in_specs=[SM] + [VM] * 11,
        out_specs=[VM, VM],
        scratch_shapes=[pltpu.VMEM((count, 2 * count), jnp.float32)],
        compiler_params=SMALL,
        name="final",
    )(me, gram, adv, *high[2:], l1, l2, l3)
    return basis, growth.reshape(count)


def solution(mesh):
    in_specs = (P("vec", None, "space", None, None), P(None, None, "space", "vec", None))
    out_specs = (P("vec", None, "space", None, None), P())
    return jax.shard_map(
        on_device, mesh=mesh, in_specs=in_specs, out_specs=out_specs, check_vma=False
    )
```

```python
import functools

import jax
import jax.numpy as jnp
from jax import lax
from jax.experimental import pallas as pl
from jax.experimental.pallas import tpu as pltpu
from jax.sharding import PartitionSpec as P

time_step = 0.1
diffusion = 0.5
VM = pl.BlockSpec(memory_space=pltpu.VMEM)
SM = pl.BlockSpec(memory_space=pltpu.SMEM)
SMALL = pltpu.CompilerParams(vmem_limit_bytes=12 * 1024 * 1024)
PARAMS = pltpu.CompilerParams(vmem_limit_bytes=20 * 1024 * 1024)
PAD = 8
CHUNK = 16


def stage_rows(src, first, bgs, bg_first, alpha, beta, keep, keep_first, rows, vectors, store):
    columns = src.shape[2] - 2 * PAD
    levels = src.shape[3]
    h = beta * time_step
    lane = lax.broadcasted_iota(jnp.int32, (CHUNK, levels), 1)

    def one_row(row, carry):
        at = row + first
        for x in range(0, columns, CHUNK):
            quarter, inner = divmod(x, bgs.shape[3])
            u, v, r, s = (
                bgs[quarter, bg_first + row, f, inner : inner + CHUNK, :].astype(jnp.float32)
                for f in range(4)
            )
            hu, hv, hr, hs = (0.5 * h) * u, (0.5 * h) * v, (0.5 * h) * r, h * s
            lap = diffusion * h
            xn_c, xp_c = lap - hu, lap + hu
            yn_c, yp_c = lap - hv, lap + hv
            zn_c = jnp.where(lane == levels - 1, 0.0, lap - hr)
            zp_c = jnp.where(lane == 0, 0.0, lap + hr)
            mid = beta - 6.0 * lap
            lo = PAD + x
            for vector in range(vectors):
                centers = [src[at, 2 * vector + f, lo : lo + CHUNK, :] for f in range(2)]
                for f in range(2):
                    k = 2 * vector + f
                    c = centers[f]
                    total = xn_c * src[at, k, lo + 1 : lo + 1 + CHUNK, :]
                    total += xp_c * src[at, k, lo - 1 : lo - 1 + CHUNK, :]
                    total += yn_c * src[at + 1, k, lo : lo + CHUNK, :]
                    total += yp_c * src[at - 1, k, lo : lo + CHUNK, :]
                    total += zn_c * pltpu.roll(c, levels - 1, 1)
                    total += zp_c * pltpu.roll(c, 1, 1)
                    total += mid * c
                    if f == 0:
                        total += h * centers[1]
                    else:
                        total -= hs * centers[0]
                    if alpha:
                        total += alpha * keep[row + keep_first, k, lo : lo + CHUNK, :]
                    store(row, vector, f, x, total)
        return carry

    lax.fori_loop(0, rows, one_row, 0)


def wrap(ref, columns):
    ref[:, :, PAD - 1 : PAD, :] = ref[:, :, PAD + columns - 1 : PAD + columns, :]
    ref[:, :, PAD + columns : PAD + columns + 1, :] = ref[:, :, PAD : PAD + 1, :]


def prep_kernel(own, narrow, last, lead):
    vectors, _, rows = own.shape[:3]
    for vector in range(vectors):
        for f in range(2):
            for row in range(rows):
                value = own[vector, f, row].astype(jnp.bfloat16)
                narrow[row, vector, f] = value
                if row == rows - 1:
                    last[vector, f] = value
                if row == 0:
                    lead[vector, f] = value


def edges_kernel(background, up, dn):
    for f in range(4):
        for row in range(2):
            up[row, f] = background[0, f, row]
            dn[row, f] = background[0, f, row]
        up[2, f] = background[1, f, 1]
        dn[2, f] = background[1, f, 0]


def pack_kernel(background, up, dn, packed):
    for f in range(4):
        for row in range(2):
            packed[row, f] = up[row, f]
            packed[2 + row, f] = background[0, f, row]
            packed[4 + row, f] = dn[row, f]
            packed[7 + row, f] = background[1, f, row]
            packed[10 + row, f] = background[2, f, row]
        packed[6, f] = up[2, f]
        packed[9, f] = dn[2, f]


def advance_kernel(me, own, up1, dn1, up2, dn2, bg0, bg1, bg2, bg3, adv, hia, hib, lo, p0, p1, p2, bg):
    vectors, _, rows, columns, _ = own.shape
    for mask, part in enumerate((bg0, bg1, bg2, bg3)):
        bg[me[0] ^ mask] = part[...]
    for vector in range(vectors):
        for f in range(2):
            k = 2 * vector + f
            cells = slice(PAD, PAD + columns)
            p0[0, k, cells, :] = up2[vector, f].astype(jnp.float32)
            p0[7, k, cells, :] = dn2[vector, f].astype(jnp.float32)
            for row in range(2):
                p0[1 + row, k, cells, :] = up1[row, vector, f].astype(jnp.float32)
                p0[3 + row, k, cells, :] = own[vector, f, row]
                p0[5 + row, k, cells, :] = dn1[row, vector, f].astype(jnp.float32)
    wrap(p0, columns)

    def to(ref):
        def store(row, vector, f, x, value):
            ref[row, 2 * vector + f, PAD + x : PAD + x + CHUNK, :] = value

        return store

    def to_out(row, vector, f, x, value):
        adv[vector, f, row, x : x + CHUNK, :] = value
        top = value.astype(jnp.bfloat16)
        hi = (hia, hib)[vector // 2]
        hi[vector % 2, f, row, x : x + CHUNK, :] = top
        lo[vector, f, row, x : x + CHUNK, :] = (value - top.astype(jnp.float32)).astype(jnp.bfloat16)

    stage_rows(p0, 1, bg, 0, 0.0, 1.0, None, 0, 6, vectors, to(p1))
    wrap(p1, columns)
    stage_rows(p1, 1, bg, 6, 0.75, 0.25, p0, 2, 4, vectors, to(p2))
    wrap(p2, columns)
    stage_rows(p2, 1, bg, 10, 1.0 / 3.0, 2.0 / 3.0, p0, 3, 2, vectors, to_out)


def stacked(blocks):
    vectors, fields, rows, columns, _ = blocks[0].shape
    parts = []
    for f in range(fields):
        for y in range(rows):
            for x in range(0, columns, CHUNK):
                parts.append(
                    jnp.concatenate(
                        [h[j, f, y, x : x + CHUNK, :] for h in blocks for j in range(vectors)]
                    )
                )
    return jnp.concatenate(parts, 1)


def pairs(left, right):
    full = lax.dot_general(left, right, (((1,), (1,)), ((), ())), preferred_element_type=jnp.float32)
    row = lax.broadcasted_iota(jnp.int32, full.shape, 0)
    lane = lax.broadcasted_iota(jnp.int32, full.shape, 1)
    full = jnp.where(row % CHUNK == lane % CHUNK, full, 0.0)
    return jnp.sum(full.reshape(full.shape[0] // CHUNK, CHUNK, full.shape[1]), axis=1)


def gram_own_kernel(h0a, h0b, h1a, h1b, out):
    flat = stacked((h0a, h0b, h1a, h1b))
    out[...] = pairs(flat, flat)


def gram_kernel(me, near, h0a, h0b, h1a, h1b, h2a, h2b, h3a, h3b, out, lines):
    vectors = 2 * h0a.shape[0]
    count = 4 * vectors
    size = count * CHUNK
    position = me[0]
    flat, other = stacked((h0a, h0b, h1a, h1b)), stacked((h2a, h2b, h3a, h3b))
    cross = pairs(flat, other)
    far = pairs(other, other)
    for b in range(2):
        for j in range(vectors):
            k = b * vectors + j
            lines[pl.ds((position ^ b) * vectors + j, 1), :] = jnp.concatenate(
                [near[k : k + 1, :], cross[k : k + 1, :]], 1
            )
            lines[pl.ds((position ^ (2 + b)) * vectors + j, 1), :] = jnp.concatenate(
                [jnp.zeros_like(far[k : k + 1, :]), far[k : k + 1, :]], 1
            )
    group = lax.broadcasted_iota(jnp.int32, (size, count), 0) // CHUNK
    target = ((group // vectors) ^ position) * vectors + group % vectors
    pick = jnp.where(target == lax.broadcasted_iota(jnp.int32, (size, count), 1), 1.0, 0.0)
    half = jnp.dot(
        lines[...], pick, precision=lax.Precision.HIGHEST, preferred_element_type=jnp.float32
    )
    row = lax.broadcasted_iota(jnp.int32, (count, count), 0) // (2 * vectors)
    lane = lax.broadcasted_iota(jnp.int32, (count, count), 1) // (2 * vectors)
    out[...] = half + jnp.where(row == lane, 0.0, half.T)


def final_kernel(scale, me, gram, own, h1a, h1b, h2a, h2b, h3a, h3b, l1, l2, l3, basis, growth, inv):
    vectors = own.shape[0]
    count = gram.shape[0]
    position = me[0]
    row = lax.broadcasted_iota(jnp.int32, (count, 2 * count), 0)
    lane = lax.broadcasted_iota(jnp.int32, (count, 2 * count), 1)
    unit = lane - count
    column = ((unit // vectors) ^ position) * vectors + unit % vectors
    eye = jnp.where((lane >= count) & (row == column), 1.0, 0.0)
    table = jnp.concatenate([gram[...] * scale, jnp.zeros((count, count), jnp.float32)], 1) + eye
    pivots = jnp.zeros((1, count), jnp.float32)
    wide = lax.broadcasted_iota(jnp.int32, (1, count), 1)
    for k in range(count):
        pivot = table[k : k + 1, k : k + 1]
        pivots = jnp.where(wide == k, pivot, pivots)
        root = lax.rsqrt(pivot)
        root = root * (1.5 - 0.5 * pivot * root * root)
        scaled = table[k : k + 1, :] * root
        below = jnp.where(row[:, :1] > k, table[:, k : k + 1] * root, 0.0)
        table = jnp.where(row == k, scaled, table - below * scaled)
    growth[...] = 0.5 * jnp.log(pivots)
    inv[...] = table
    for first in range(0, vectors, 2):
        weights = []
        for i in range(first, first + 2):
            line = inv[pl.ds(position * vectors + i, 1), :]
            weights.append(
                [
                    jnp.broadcast_to(line[:, count + j : count + j + 1], (CHUNK, own.shape[4]))
                    for j in range(count)
                ]
            )
        for f in range(own.shape[1]):
            for y in range(own.shape[2]):

                def tile(t, carry, f=f, y=y, first=first, weights=weights):
                    at = pl.ds(pl.multiple_of(t * CHUNK, CHUNK), CHUNK)
                    values = [own[j, f, y, at, :] for j in range(vectors)]
                    for h, l in (((h1a, h1b), l1), ((h2a, h2b), l2), ((h3a, h3b), l3)):
                        for j in range(vectors):
                            values.append(
                                h[j // 2][j % 2, f, y, at, :].astype(jnp.float32)
                                + l[j, f, y, at, :].astype(jnp.float32)
                            )
                    for i in range(2):
                        parts = [w * value for w, value in zip(weights[i], values)]
                        while len(parts) > 1:
                            parts = [a + b for a, b in zip(parts[::2], parts[1::2])]
                        basis[first + i, f, y, at, :] = parts[0]
                    return carry

                lax.fori_loop(0, own.shape[3] // CHUNK, tile, 0, unroll=2)


def shift(value, axis, step):
    count = lax.axis_size(axis)
    return lax.ppermute(value, axis, [(i, (i + step) % count) for i in range(count)])


def swap(value, axis, mask):
    return lax.ppermute(value, axis, [(i, i ^ mask) for i in range(lax.axis_size(axis))])


def on_device(tangents, background):
    vectors, fields, rows, columns, levels = tangents.shape
    count = vectors * lax.axis_size("vec")
    cells = fields * rows * columns * levels * lax.axis_size("space")
    me = lax.axis_index("vec").astype(jnp.int32).reshape(1)

    row_shape = jax.ShapeDtypeStruct((vectors, fields, columns, levels), jnp.bfloat16)
    narrow, last, lead = pl.pallas_call(
        prep_kernel,
        out_shape=[jax.ShapeDtypeStruct((rows,) + row_shape.shape, jnp.bfloat16), row_shape, row_shape],
        in_specs=[VM],
        out_specs=[VM] * 3,
        compiler_params=SMALL,
        name="prep",
    )(tangents)
    edge = jax.ShapeDtypeStruct((3, 4) + background.shape[3:], jnp.bfloat16)
    bg_up, bg_dn = pl.pallas_call(
        edges_kernel,
        out_shape=[edge, edge],
        in_specs=[VM],
        out_specs=[VM] * 2,
        compiler_params=SMALL,
        name="edges",
    )(background)
    bg_up = shift(bg_up, "space", 1)
    bg_dn = shift(bg_dn, "space", -1)
    narrow, last, lead, bg_up, bg_dn = lax.optimization_barrier((narrow, last, lead, bg_up, bg_dn))
    up1 = shift(narrow, "space", 1)
    dn1 = shift(narrow, "space", -1)
    up2 = shift(last, "space", 2)
    dn2 = shift(lead, "space", -2)
    packed = pl.pallas_call(
        pack_kernel,
        out_shape=jax.ShapeDtypeStruct((12, 4) + background.shape[3:], jnp.bfloat16),
        in_specs=[VM] * 3,
        out_specs=VM,
        compiler_params=SMALL,
        name="pack",
    )(background, bg_up, bg_dn)
    bg2 = swap(packed, "vec", 2)
    near_bg, far_bg, up2, dn2 = lax.optimization_barrier((packed, bg2, up2, dn2))
    bgs = [packed, swap(near_bg, "vec", 1), bg2, swap(far_bg, "vec", 1)]

    low = jax.ShapeDtypeStruct(tangents.shape, jnp.bfloat16)
    pair = jax.ShapeDtypeStruct((vectors // 2,) + tangents.shape[1:], jnp.bfloat16)
    fields_all = 2 * vectors
    adv, hia, hib, lo = pl.pallas_call(
        advance_kernel,
        out_shape=[jax.ShapeDtypeStruct(tangents.shape, jnp.float32), pair, pair, low],
        in_specs=[SM] + [VM] * 9,
        out_specs=[VM] * 4,
        scratch_shapes=[
            pltpu.VMEM((8, fields_all, columns + 2 * PAD, levels), jnp.float32),
            pltpu.VMEM((6, fields_all, columns + 2 * PAD, levels), jnp.float32),
            pltpu.VMEM((4, fields_all, columns + 2 * PAD, levels), jnp.float32),
            pltpu.VMEM((4,) + packed.shape, jnp.bfloat16),
            ],
        compiler_params=PARAMS,
        name="advance",
    )(me, tangents, up1, dn1, up2, dn2, *bgs)

    h2a, h1a = swap(hia, "vec", 2), swap(hia, "vec", 1)
    h2b, h1b = swap(hib, "vec", 2), swap(hib, "vec", 1)
    near = pl.pallas_call(
        gram_own_kernel,
        out_shape=jax.ShapeDtypeStruct((2 * vectors, 2 * vectors * CHUNK), jnp.float32),
        in_specs=[VM] * 4,
        out_specs=VM,
        compiler_params=SMALL,
        name="gram_own",
    )(hia, hib, h1a, h1b)
    lo, near = lax.optimization_barrier((lo, near))
    l2, l1 = swap(lo, "vec", 2), swap(lo, "vec", 1)
    h3a, h3b = swap(h2a, "vec", 1), swap(h2b, "vec", 1)
    high = (hia, hib, h1a, h1b, h2a, h2b, h3a, h3b)

    gram = pl.pallas_call(
        gram_kernel,
        out_shape=jax.ShapeDtypeStruct((count, count), jnp.float32),
        in_specs=[SM] + [VM] * 9,
        out_specs=VM,
        scratch_shapes=[pltpu.VMEM((count, count * CHUNK), jnp.float32)],
        compiler_params=SMALL,
        name="gram",
    )(me, near, *high)
    mask, size = 1, lax.axis_size("space")
    while mask < size:
        if 2 * mask >= size:
            gram, l2 = lax.optimization_barrier((gram, l2))
            l3 = swap(l2, "vec", 1)
        gram = gram + swap(gram, "space", mask)
        mask *= 2

    basis, growth = pl.pallas_call(
        functools.partial(final_kernel, 1.0 / cells),
        out_shape=[
            jax.ShapeDtypeStruct(tangents.shape, jnp.float32),
            jax.ShapeDtypeStruct((1, count), jnp.float32),
        ],
        in_specs=[SM] + [VM] * 11,
        out_specs=[VM, VM],
        scratch_shapes=[pltpu.VMEM((count, 2 * count), jnp.float32)],
        compiler_params=SMALL,
        name="final",
    )(me, gram, adv, *high[2:], l1, l2, l3)
    return basis, growth.reshape(count)


def solution(mesh):
    in_specs = (P("vec", None, "space", None, None), P(None, None, "space", "vec", None))
    out_specs = (P("vec", None, "space", None, None), P())
    return jax.shard_map(
        on_device, mesh=mesh, in_specs=in_specs, out_specs=out_specs, check_vma=False
    )
```

```python
import functools

import jax
import jax.numpy as jnp
from jax import lax
from jax.experimental import pallas as pl
from jax.experimental.pallas import tpu as pltpu
from jax.sharding import PartitionSpec as P

time_step = 0.1
diffusion = 0.5
VM = pl.BlockSpec(memory_space=pltpu.VMEM)
SM = pl.BlockSpec(memory_space=pltpu.SMEM)
SMALL = pltpu.CompilerParams(vmem_limit_bytes=12 * 1024 * 1024)
PARAMS = pltpu.CompilerParams(vmem_limit_bytes=20 * 1024 * 1024)
PAD = 8
CHUNK = 16


def stage_rows(src, first, bgs, bg_first, alpha, beta, keep, keep_first, rows, vectors, store):
    columns = src.shape[2] - 2 * PAD
    levels = src.shape[3]
    h = beta * time_step
    lane = lax.broadcasted_iota(jnp.int32, (CHUNK, levels), 1)

    def one_row(row, carry):
        at = row + first
        for x in range(0, columns, CHUNK):
            quarter, inner = divmod(x, bgs.shape[3])
            u, v, r, s = (
                bgs[quarter, bg_first + row, f, inner : inner + CHUNK, :].astype(jnp.float32)
                for f in range(4)
            )
            hu, hv, hr, hs = (0.5 * h) * u, (0.5 * h) * v, (0.5 * h) * r, h * s
            lap = diffusion * h
            xn_c, xp_c = lap - hu, lap + hu
            yn_c, yp_c = lap - hv, lap + hv
            zn_c = jnp.where(lane == levels - 1, 0.0, lap - hr)
            zp_c = jnp.where(lane == 0, 0.0, lap + hr)
            mid = beta - 6.0 * lap
            lo = PAD + x
            for vector in range(vectors):
                centers = [src[at, 2 * vector + f, lo : lo + CHUNK, :] for f in range(2)]
                for f in range(2):
                    k = 2 * vector + f
                    c = centers[f]
                    total = xn_c * src[at, k, lo + 1 : lo + 1 + CHUNK, :]
                    total += xp_c * src[at, k, lo - 1 : lo - 1 + CHUNK, :]
                    total += yn_c * src[at + 1, k, lo : lo + CHUNK, :]
                    total += yp_c * src[at - 1, k, lo : lo + CHUNK, :]
                    total += zn_c * pltpu.roll(c, levels - 1, 1)
                    total += zp_c * pltpu.roll(c, 1, 1)
                    total += mid * c
                    if f == 0:
                        total += h * centers[1]
                    else:
                        total -= hs * centers[0]
                    if alpha:
                        total += alpha * keep[row + keep_first, k, lo : lo + CHUNK, :]
                    store(row, vector, f, x, total)
        return carry

    lax.fori_loop(0, rows, one_row, 0)


def wrap(ref, columns):
    ref[:, :, PAD - 1 : PAD, :] = ref[:, :, PAD + columns - 1 : PAD + columns, :]
    ref[:, :, PAD + columns : PAD + columns + 1, :] = ref[:, :, PAD : PAD + 1, :]


def prep_kernel(own, narrow, last, lead):
    vectors, _, rows = own.shape[:3]
    for vector in range(vectors):
        for f in range(2):
            for row in range(rows):
                value = own[vector, f, row].astype(jnp.bfloat16)
                narrow[row, vector, f] = value
                if row == rows - 1:
                    last[vector, f] = value
                if row == 0:
                    lead[vector, f] = value


def edges_kernel(background, up, dn):
    for f in range(4):
        for row in range(2):
            up[row, f] = background[0, f, row]
            dn[row, f] = background[0, f, row]
        up[2, f] = background[1, f, 1]
        dn[2, f] = background[1, f, 0]


def pack_kernel(background, up, dn, packed):
    for f in range(4):
        for row in range(2):
            packed[row, f] = up[row, f]
            packed[2 + row, f] = background[0, f, row]
            packed[4 + row, f] = dn[row, f]
            packed[7 + row, f] = background[1, f, row]
            packed[10 + row, f] = background[2, f, row]
        packed[6, f] = up[2, f]
        packed[9, f] = dn[2, f]


def advance_kernel(me, own, up1, dn1, up2, dn2, bg0, bg1, bg2, bg3, adv, hia, hib, lo, p0, p1, p2, bg):
    vectors, _, rows, columns, _ = own.shape
    for mask, part in enumerate((bg0, bg1, bg2, bg3)):
        bg[me[0] ^ mask] = part[...]
    for vector in range(vectors):
        for f in range(2):
            k = 2 * vector + f
            cells = slice(PAD, PAD + columns)
            p0[0, k, cells, :] = up2[vector, f].astype(jnp.float32)
            p0[7, k, cells, :] = dn2[vector, f].astype(jnp.float32)
            for row in range(2):
                p0[1 + row, k, cells, :] = up1[row, vector, f].astype(jnp.float32)
                p0[3 + row, k, cells, :] = own[vector, f, row]
                p0[5 + row, k, cells, :] = dn1[row, vector, f].astype(jnp.float32)
    wrap(p0, columns)

    def to(ref):
        def store(row, vector, f, x, value):
            ref[row, 2 * vector + f, PAD + x : PAD + x + CHUNK, :] = value

        return store

    def to_out(row, vector, f, x, value):
        adv[vector, f, row, x : x + CHUNK, :] = value
        top = value.astype(jnp.bfloat16)
        hi = (hia, hib)[vector // 2]
        hi[vector % 2, f, row, x : x + CHUNK, :] = top
        lo[vector, f, row, x : x + CHUNK, :] = (value - top.astype(jnp.float32)).astype(jnp.bfloat16)

    stage_rows(p0, 1, bg, 0, 0.0, 1.0, None, 0, 6, vectors, to(p1))
    wrap(p1, columns)
    stage_rows(p1, 1, bg, 6, 0.75, 0.25, p0, 2, 4, vectors, to(p2))
    wrap(p2, columns)
    stage_rows(p2, 1, bg, 10, 1.0 / 3.0, 2.0 / 3.0, p0, 3, 2, vectors, to_out)


def stacked(blocks):
    vectors, fields, rows, columns, _ = blocks[0].shape
    parts = []
    for f in range(fields):
        for y in range(rows):
            for x in range(0, columns, CHUNK):
                parts.append(
                    jnp.concatenate(
                        [h[j, f, y, x : x + CHUNK, :] for h in blocks for j in range(vectors)]
                    )
                )
    return jnp.concatenate(parts, 1)


def pairs(left, right):
    full = lax.dot_general(left, right, (((1,), (1,)), ((), ())), preferred_element_type=jnp.float32)
    row = lax.broadcasted_iota(jnp.int32, full.shape, 0)
    lane = lax.broadcasted_iota(jnp.int32, full.shape, 1)
    full = jnp.where(row % CHUNK == lane % CHUNK, full, 0.0)
    return jnp.sum(full.reshape(full.shape[0] // CHUNK, CHUNK, full.shape[1]), axis=1)


def gram_own_kernel(h0a, h0b, h1a, h1b, out):
    flat = stacked((h0a, h0b, h1a, h1b))
    out[...] = pairs(flat, flat)


def gram_kernel(me, near, h0a, h0b, h1a, h1b, h2a, h2b, h3a, h3b, out, lines):
    vectors = 2 * h0a.shape[0]
    count = 4 * vectors
    size = count * CHUNK
    position = me[0]
    flat, other = stacked((h0a, h0b, h1a, h1b)), stacked((h2a, h2b, h3a, h3b))
    cross = pairs(flat, other)
    far = pairs(other, other)
    for b in range(2):
        for j in range(vectors):
            k = b * vectors + j
            lines[pl.ds((position ^ b) * vectors + j, 1), :] = jnp.concatenate(
                [near[k : k + 1, :], cross[k : k + 1, :]], 1
            )
            lines[pl.ds((position ^ (2 + b)) * vectors + j, 1), :] = jnp.concatenate(
                [jnp.zeros_like(far[k : k + 1, :]), far[k : k + 1, :]], 1
            )
    group = lax.broadcasted_iota(jnp.int32, (size, count), 0) // CHUNK
    target = ((group // vectors) ^ position) * vectors + group % vectors
    pick = jnp.where(target == lax.broadcasted_iota(jnp.int32, (size, count), 1), 1.0, 0.0)
    half = jnp.dot(
        lines[...], pick, precision=lax.Precision.HIGHEST, preferred_element_type=jnp.float32
    )
    row = lax.broadcasted_iota(jnp.int32, (count, count), 0) // (2 * vectors)
    lane = lax.broadcasted_iota(jnp.int32, (count, count), 1) // (2 * vectors)
    out[...] = half + jnp.where(row == lane, 0.0, half.T)


def final_kernel(scale, me, gram, own, h1a, h1b, h2a, h2b, h3a, h3b, l1, l2, l3, basis, growth, inv):
    vectors = own.shape[0]
    count = gram.shape[0]
    position = me[0]
    levels = own.shape[4]
    scaled = gram[...] * scale
    left = [jnp.broadcast_to(scaled[:, i : i + 1], (count, levels)) for i in range(count)]
    unit = lax.broadcasted_iota(jnp.int32, (count, levels), 0)
    column = ((unit // vectors) ^ position) * vectors + unit % vectors
    right = [jnp.where(column == i, 1.0, 0.0) for i in range(count)]
    wide = lax.broadcasted_iota(jnp.int32, (1, levels), 1)
    pivots = jnp.ones((1, levels), jnp.float32)
    for k in range(count):
        pivot = left[k][k : k + 1, :]
        pivots = jnp.where(wide == k, pivot, pivots)
        turn = 1.0 / pivot
        line, unit_line = left[k] * turn, right[k] * turn
        for i in range(k + 1, count):
            factor = left[i][k : k + 1, :]
            left[i] = left[i] - factor * line
            right[i] = right[i] - factor * unit_line
        inv[k] = right[k] / jnp.sqrt(pivot)
    growth[...] = (0.5 * jnp.log(pivots))[:, :count]
    for first in range(0, vectors, 2):
        weights = []
        for i in range(first, first + 2):
            line = inv[position * vectors + i]
            weights.append(
                [
                    jnp.broadcast_to(line[j : j + 1, :], (CHUNK, levels))
                    for j in range(count)
                ]
            )
        for f in range(own.shape[1]):
            for y in range(own.shape[2]):

                def tile(t, carry, f=f, y=y, first=first, weights=weights):
                    at = pl.ds(pl.multiple_of(t * CHUNK, CHUNK), CHUNK)
                    values = [own[j, f, y, at, :] for j in range(vectors)]
                    for h, l in (((h1a, h1b), l1), ((h2a, h2b), l2), ((h3a, h3b), l3)):
                        for j in range(vectors):
                            values.append(
                                h[j // 2][j % 2, f, y, at, :].astype(jnp.float32)
                                + l[j, f, y, at, :].astype(jnp.float32)
                            )
                    for i in range(2):
                        parts = [w * value for w, value in zip(weights[i], values)]
                        while len(parts) > 1:
                            parts = [a + b for a, b in zip(parts[::2], parts[1::2])]
                        basis[first + i, f, y, at, :] = parts[0]
                    return carry

                lax.fori_loop(0, own.shape[3] // CHUNK, tile, 0, unroll=2)


def shift(value, axis, step):
    count = lax.axis_size(axis)
    return lax.ppermute(value, axis, [(i, (i + step) % count) for i in range(count)])


def swap(value, axis, mask):
    return lax.ppermute(value, axis, [(i, i ^ mask) for i in range(lax.axis_size(axis))])


def on_device(tangents, background):
    vectors, fields, rows, columns, levels = tangents.shape
    count = vectors * lax.axis_size("vec")
    cells = fields * rows * columns * levels * lax.axis_size("space")
    me = lax.axis_index("vec").astype(jnp.int32).reshape(1)

    row_shape = jax.ShapeDtypeStruct((vectors, fields, columns, levels), jnp.bfloat16)
    narrow, last, lead = pl.pallas_call(
        prep_kernel,
        out_shape=[jax.ShapeDtypeStruct((rows,) + row_shape.shape, jnp.bfloat16), row_shape, row_shape],
        in_specs=[VM],
        out_specs=[VM] * 3,
        compiler_params=SMALL,
        name="prep",
    )(tangents)
    edge = jax.ShapeDtypeStruct((3, 4) + background.shape[3:], jnp.bfloat16)
    bg_up, bg_dn = pl.pallas_call(
        edges_kernel,
        out_shape=[edge, edge],
        in_specs=[VM],
        out_specs=[VM] * 2,
        compiler_params=SMALL,
        name="edges",
    )(background)
    bg_up = shift(bg_up, "space", 1)
    bg_dn = shift(bg_dn, "space", -1)
    narrow, last, lead, bg_up, bg_dn = lax.optimization_barrier((narrow, last, lead, bg_up, bg_dn))
    up1 = shift(narrow, "space", 1)
    dn1 = shift(narrow, "space", -1)
    up2 = shift(last, "space", 2)
    dn2 = shift(lead, "space", -2)
    packed = pl.pallas_call(
        pack_kernel,
        out_shape=jax.ShapeDtypeStruct((12, 4) + background.shape[3:], jnp.bfloat16),
        in_specs=[VM] * 3,
        out_specs=VM,
        compiler_params=SMALL,
        name="pack",
    )(background, bg_up, bg_dn)
    bg2 = swap(packed, "vec", 2)
    near_bg, far_bg, up2, dn2 = lax.optimization_barrier((packed, bg2, up2, dn2))
    bgs = [packed, swap(near_bg, "vec", 1), bg2, swap(far_bg, "vec", 1)]

    low = jax.ShapeDtypeStruct(tangents.shape, jnp.bfloat16)
    pair = jax.ShapeDtypeStruct((vectors // 2,) + tangents.shape[1:], jnp.bfloat16)
    fields_all = 2 * vectors
    adv, hia, hib, lo = pl.pallas_call(
        advance_kernel,
        out_shape=[jax.ShapeDtypeStruct(tangents.shape, jnp.float32), pair, pair, low],
        in_specs=[SM] + [VM] * 9,
        out_specs=[VM] * 4,
        scratch_shapes=[
            pltpu.VMEM((8, fields_all, columns + 2 * PAD, levels), jnp.float32),
            pltpu.VMEM((6, fields_all, columns + 2 * PAD, levels), jnp.float32),
            pltpu.VMEM((4, fields_all, columns + 2 * PAD, levels), jnp.float32),
            pltpu.VMEM((4,) + packed.shape, jnp.bfloat16),
            ],
        compiler_params=PARAMS,
        name="advance",
    )(me, tangents, up1, dn1, up2, dn2, *bgs)

    h2a, h1a = swap(hia, "vec", 2), swap(hia, "vec", 1)
    h2b, h1b = swap(hib, "vec", 2), swap(hib, "vec", 1)
    near = pl.pallas_call(
        gram_own_kernel,
        out_shape=jax.ShapeDtypeStruct((2 * vectors, 2 * vectors * CHUNK), jnp.float32),
        in_specs=[VM] * 4,
        out_specs=VM,
        compiler_params=SMALL,
        name="gram_own",
    )(hia, hib, h1a, h1b)
    lo, near = lax.optimization_barrier((lo, near))
    l2, l1 = swap(lo, "vec", 2), swap(lo, "vec", 1)
    h3a, h3b = swap(h2a, "vec", 1), swap(h2b, "vec", 1)
    high = (hia, hib, h1a, h1b, h2a, h2b, h3a, h3b)

    gram = pl.pallas_call(
        gram_kernel,
        out_shape=jax.ShapeDtypeStruct((count, count), jnp.float32),
        in_specs=[SM] + [VM] * 9,
        out_specs=VM,
        scratch_shapes=[pltpu.VMEM((count, count * CHUNK), jnp.float32)],
        compiler_params=SMALL,
        name="gram",
    )(me, near, *high)
    mask, size = 1, lax.axis_size("space")
    while mask < size:
        if 2 * mask >= size:
            gram, l2 = lax.optimization_barrier((gram, l2))
            l3 = swap(l2, "vec", 1)
        gram = gram + swap(gram, "space", mask)
        mask *= 2

    basis, growth = pl.pallas_call(
        functools.partial(final_kernel, 1.0 / cells),
        out_shape=[
            jax.ShapeDtypeStruct(tangents.shape, jnp.float32),
            jax.ShapeDtypeStruct((1, count), jnp.float32),
        ],
        in_specs=[SM] + [VM] * 11,
        out_specs=[VM, VM],
        scratch_shapes=[pltpu.VMEM((count, count, levels), jnp.float32)],
        compiler_params=SMALL,
        name="final",
    )(me, gram, adv, *high[2:], l1, l2, l3)
    return basis, growth.reshape(count)


def solution(mesh):
    in_specs = (P("vec", None, "space", None, None), P(None, None, "space", "vec", None))
    out_specs = (P("vec", None, "space", None, None), P())
    return jax.shard_map(
        on_device, mesh=mesh, in_specs=in_specs, out_specs=out_specs, check_vma=False
    )
```

```python
import functools

import jax
import jax.numpy as jnp
from jax import lax
from jax.experimental import pallas as pl
from jax.experimental.pallas import tpu as pltpu
from jax.sharding import PartitionSpec as P

time_step = 0.1
diffusion = 0.5
VM = pl.BlockSpec(memory_space=pltpu.VMEM)
SM = pl.BlockSpec(memory_space=pltpu.SMEM)
SMALL = pltpu.CompilerParams(vmem_limit_bytes=12 * 1024 * 1024)
PARAMS = pltpu.CompilerParams(vmem_limit_bytes=20 * 1024 * 1024)
PAD = 8
CHUNK = 16


def stage_rows(src, first, bgs, bg_first, alpha, beta, keep, keep_first, rows, vectors, store):
    columns = src.shape[2] - 2 * PAD
    levels = src.shape[3]
    h = beta * time_step
    lane = lax.broadcasted_iota(jnp.int32, (CHUNK, levels), 1)

    def one_row(row, carry):
        at = row + first
        for x in range(0, columns, CHUNK):
            quarter, inner = divmod(x, bgs.shape[3])
            u, v, r, s = (
                bgs[quarter, bg_first + row, f, inner : inner + CHUNK, :].astype(jnp.float32)
                for f in range(4)
            )
            hu, hv, hr, hs = (0.5 * h) * u, (0.5 * h) * v, (0.5 * h) * r, h * s
            lap = diffusion * h
            xn_c, xp_c = lap - hu, lap + hu
            yn_c, yp_c = lap - hv, lap + hv
            zn_c = jnp.where(lane == levels - 1, 0.0, lap - hr)
            zp_c = jnp.where(lane == 0, 0.0, lap + hr)
            mid = beta - 6.0 * lap
            lo = PAD + x
            for vector in range(vectors):
                centers = [src[at, 2 * vector + f, lo : lo + CHUNK, :] for f in range(2)]
                for f in range(2):
                    k = 2 * vector + f
                    c = centers[f]
                    total = xn_c * src[at, k, lo + 1 : lo + 1 + CHUNK, :]
                    total += xp_c * src[at, k, lo - 1 : lo - 1 + CHUNK, :]
                    total += yn_c * src[at + 1, k, lo : lo + CHUNK, :]
                    total += yp_c * src[at - 1, k, lo : lo + CHUNK, :]
                    total += zn_c * pltpu.roll(c, levels - 1, 1)
                    total += zp_c * pltpu.roll(c, 1, 1)
                    total += mid * c
                    if f == 0:
                        total += h * centers[1]
                    else:
                        total -= hs * centers[0]
                    if alpha:
                        total += alpha * keep[row + keep_first, k, lo : lo + CHUNK, :]
                    store(row, vector, f, x, total)
        return carry

    lax.fori_loop(0, rows, one_row, 0, unroll=2)


def wrap(ref, columns):
    ref[:, :, PAD - 1 : PAD, :] = ref[:, :, PAD + columns - 1 : PAD + columns, :]
    ref[:, :, PAD + columns : PAD + columns + 1, :] = ref[:, :, PAD : PAD + 1, :]


def prep_kernel(own, narrow, last, lead):
    vectors, _, rows = own.shape[:3]
    for vector in range(vectors):
        for f in range(2):
            for row in range(rows):
                value = own[vector, f, row].astype(jnp.bfloat16)
                narrow[row, vector, f] = value
                if row == rows - 1:
                    last[vector, f] = value
                if row == 0:
                    lead[vector, f] = value


def edges_kernel(background, up, dn):
    for f in range(4):
        for row in range(2):
            up[row, f] = background[0, f, row]
            dn[row, f] = background[0, f, row]
        up[2, f] = background[1, f, 1]
        dn[2, f] = background[1, f, 0]


def pack_kernel(background, up, dn, packed):
    for f in range(4):
        for row in range(2):
            packed[row, f] = up[row, f]
            packed[2 + row, f] = background[0, f, row]
            packed[4 + row, f] = dn[row, f]
            packed[7 + row, f] = background[1, f, row]
            packed[10 + row, f] = background[2, f, row]
        packed[6, f] = up[2, f]
        packed[9, f] = dn[2, f]


def advance_kernel(me, own, up1, dn1, up2, dn2, bg0, bg1, bg2, bg3, adv, hia, hib, lo, p0, p1, p2, bg):
    vectors, _, rows, columns, _ = own.shape
    for mask, part in enumerate((bg0, bg1, bg2, bg3)):
        bg[me[0] ^ mask] = part[...]
    for vector in range(vectors):
        for f in range(2):
            k = 2 * vector + f
            cells = slice(PAD, PAD + columns)
            p0[0, k, cells, :] = up2[vector, f].astype(jnp.float32)
            p0[7, k, cells, :] = dn2[vector, f].astype(jnp.float32)
            for row in range(2):
                p0[1 + row, k, cells, :] = up1[row, vector, f].astype(jnp.float32)
                p0[3 + row, k, cells, :] = own[vector, f, row]
                p0[5 + row, k, cells, :] = dn1[row, vector, f].astype(jnp.float32)
    wrap(p0, columns)

    def to(ref):
        def store(row, vector, f, x, value):
            ref[row, 2 * vector + f, PAD + x : PAD + x + CHUNK, :] = value

        return store

    def to_out(row, vector, f, x, value):
        adv[vector, f, row, x : x + CHUNK, :] = value
        top = value.astype(jnp.bfloat16)
        hi = (hia, hib)[vector // 2]
        hi[vector % 2, f, row, x : x + CHUNK, :] = top
        lo[vector, f, row, x : x + CHUNK, :] = (value - top.astype(jnp.float32)).astype(jnp.bfloat16)

    stage_rows(p0, 1, bg, 0, 0.0, 1.0, None, 0, 6, vectors, to(p1))
    wrap(p1, columns)
    stage_rows(p1, 1, bg, 6, 0.75, 0.25, p0, 2, 4, vectors, to(p2))
    wrap(p2, columns)
    stage_rows(p2, 1, bg, 10, 1.0 / 3.0, 2.0 / 3.0, p0, 3, 2, vectors, to_out)


def stacked(blocks):
    vectors, fields, rows, columns, _ = blocks[0].shape
    parts = []
    for f in range(fields):
        for y in range(rows):
            for x in range(0, columns, CHUNK):
                parts.append(
                    jnp.concatenate(
                        [h[j, f, y, x : x + CHUNK, :] for h in blocks for j in range(vectors)]
                    )
                )
    return jnp.concatenate(parts, 1)


def pairs(left, right):
    full = lax.dot_general(left, right, (((1,), (1,)), ((), ())), preferred_element_type=jnp.float32)
    row = lax.broadcasted_iota(jnp.int32, full.shape, 0)
    lane = lax.broadcasted_iota(jnp.int32, full.shape, 1)
    full = jnp.where(row % CHUNK == lane % CHUNK, full, 0.0)
    return jnp.sum(full.reshape(full.shape[0] // CHUNK, CHUNK, full.shape[1]), axis=1)


def gram_own_kernel(h0a, h0b, h1a, h1b, out):
    flat = stacked((h0a, h0b, h1a, h1b))
    out[...] = pairs(flat, flat)


def gram_kernel(me, near, h0a, h0b, h1a, h1b, h2a, h2b, h3a, h3b, out, lines):
    vectors = 2 * h0a.shape[0]
    count = 4 * vectors
    size = count * CHUNK
    position = me[0]
    flat, other = stacked((h0a, h0b, h1a, h1b)), stacked((h2a, h2b, h3a, h3b))
    cross = pairs(flat, other)
    far = pairs(other, other)
    for b in range(2):
        for j in range(vectors):
            k = b * vectors + j
            lines[pl.ds((position ^ b) * vectors + j, 1), :] = jnp.concatenate(
                [near[k : k + 1, :], cross[k : k + 1, :]], 1
            )
            lines[pl.ds((position ^ (2 + b)) * vectors + j, 1), :] = jnp.concatenate(
                [jnp.zeros_like(far[k : k + 1, :]), far[k : k + 1, :]], 1
            )
    group = lax.broadcasted_iota(jnp.int32, (size, count), 0) // CHUNK
    target = ((group // vectors) ^ position) * vectors + group % vectors
    pick = jnp.where(target == lax.broadcasted_iota(jnp.int32, (size, count), 1), 1.0, 0.0)
    half = jnp.dot(
        lines[...], pick, precision=lax.Precision.HIGHEST, preferred_element_type=jnp.float32
    )
    row = lax.broadcasted_iota(jnp.int32, (count, count), 0) // (2 * vectors)
    lane = lax.broadcasted_iota(jnp.int32, (count, count), 1) // (2 * vectors)
    out[...] = half + jnp.where(row == lane, 0.0, half.T)


def final_kernel(scale, me, gram, own, h1a, h1b, h2a, h2b, h3a, h3b, l1, l2, l3, basis, growth, inv):
    vectors = own.shape[0]
    count = gram.shape[0]
    position = me[0]
    levels = own.shape[4]
    scaled = gram[...] * scale
    left = [jnp.broadcast_to(scaled[:, i : i + 1], (count, levels)) for i in range(count)]
    unit = lax.broadcasted_iota(jnp.int32, (count, levels), 0)
    column = ((unit // vectors) ^ position) * vectors + unit % vectors
    right = [jnp.where(column == i, 1.0, 0.0) for i in range(count)]
    wide = lax.broadcasted_iota(jnp.int32, (1, levels), 1)
    pivots = jnp.ones((1, levels), jnp.float32)
    for k in range(count):
        pivot = left[k][k : k + 1, :]
        pivots = jnp.where(wide == k, pivot, pivots)
        turn = 1.0 / pivot
        line, unit_line = left[k] * turn, right[k] * turn
        for i in range(k + 1, count):
            factor = left[i][k : k + 1, :]
            left[i] = left[i] - factor * line
            right[i] = right[i] - factor * unit_line
        inv[k] = right[k] / jnp.sqrt(pivot)
    growth[...] = (0.5 * jnp.log(pivots))[:, :count]
    for first in range(0, vectors, 2):
        weights = []
        for i in range(first, first + 2):
            line = inv[position * vectors + i]
            weights.append(
                [
                    jnp.broadcast_to(line[j : j + 1, :], (CHUNK, levels))
                    for j in range(count)
                ]
            )
        for f in range(own.shape[1]):
            for y in range(own.shape[2]):

                def tile(t, carry, f=f, y=y, first=first, weights=weights):
                    at = pl.ds(pl.multiple_of(t * CHUNK, CHUNK), CHUNK)
                    values = [own[j, f, y, at, :] for j in range(vectors)]
                    for h, l in (((h1a, h1b), l1), ((h2a, h2b), l2), ((h3a, h3b), l3)):
                        for j in range(vectors):
                            values.append(
                                h[j // 2][j % 2, f, y, at, :].astype(jnp.float32)
                                + l[j, f, y, at, :].astype(jnp.float32)
                            )
                    for i in range(2):
                        parts = [w * value for w, value in zip(weights[i], values)]
                        while len(parts) > 1:
                            parts = [a + b for a, b in zip(parts[::2], parts[1::2])]
                        basis[first + i, f, y, at, :] = parts[0]
                    return carry

                lax.fori_loop(0, own.shape[3] // CHUNK, tile, 0, unroll=2)


def shift(value, axis, step):
    count = lax.axis_size(axis)
    return lax.ppermute(value, axis, [(i, (i + step) % count) for i in range(count)])


def swap(value, axis, mask):
    return lax.ppermute(value, axis, [(i, i ^ mask) for i in range(lax.axis_size(axis))])


def on_device(tangents, background):
    vectors, fields, rows, columns, levels = tangents.shape
    count = vectors * lax.axis_size("vec")
    cells = fields * rows * columns * levels * lax.axis_size("space")
    me = lax.axis_index("vec").astype(jnp.int32).reshape(1)

    row_shape = jax.ShapeDtypeStruct((vectors, fields, columns, levels), jnp.bfloat16)
    narrow, last, lead = pl.pallas_call(
        prep_kernel,
        out_shape=[jax.ShapeDtypeStruct((rows,) + row_shape.shape, jnp.bfloat16), row_shape, row_shape],
        in_specs=[VM],
        out_specs=[VM] * 3,
        compiler_params=SMALL,
        name="prep",
    )(tangents)
    edge = jax.ShapeDtypeStruct((3, 4) + background.shape[3:], jnp.bfloat16)
    bg_up, bg_dn = pl.pallas_call(
        edges_kernel,
        out_shape=[edge, edge],
        in_specs=[VM],
        out_specs=[VM] * 2,
        compiler_params=SMALL,
        name="edges",
    )(background)
    bg_up = shift(bg_up, "space", 1)
    bg_dn = shift(bg_dn, "space", -1)
    narrow, last, lead, bg_up, bg_dn = lax.optimization_barrier((narrow, last, lead, bg_up, bg_dn))
    up1 = shift(narrow, "space", 1)
    dn1 = shift(narrow, "space", -1)
    up2 = shift(last, "space", 2)
    dn2 = shift(lead, "space", -2)
    packed = pl.pallas_call(
        pack_kernel,
        out_shape=jax.ShapeDtypeStruct((12, 4) + background.shape[3:], jnp.bfloat16),
        in_specs=[VM] * 3,
        out_specs=VM,
        compiler_params=SMALL,
        name="pack",
    )(background, bg_up, bg_dn)
    bg2 = swap(packed, "vec", 2)
    near_bg, far_bg, up2, dn2 = lax.optimization_barrier((packed, bg2, up2, dn2))
    bgs = [packed, swap(near_bg, "vec", 1), bg2, swap(far_bg, "vec", 1)]

    low = jax.ShapeDtypeStruct(tangents.shape, jnp.bfloat16)
    pair = jax.ShapeDtypeStruct((vectors // 2,) + tangents.shape[1:], jnp.bfloat16)
    fields_all = 2 * vectors
    adv, hia, hib, lo = pl.pallas_call(
        advance_kernel,
        out_shape=[jax.ShapeDtypeStruct(tangents.shape, jnp.float32), pair, pair, low],
        in_specs=[SM] + [VM] * 9,
        out_specs=[VM] * 4,
        scratch_shapes=[
            pltpu.VMEM((8, fields_all, columns + 2 * PAD, levels), jnp.float32),
            pltpu.VMEM((6, fields_all, columns + 2 * PAD, levels), jnp.float32),
            pltpu.VMEM((4, fields_all, columns + 2 * PAD, levels), jnp.float32),
            pltpu.VMEM((4,) + packed.shape, jnp.bfloat16),
            ],
        compiler_params=PARAMS,
        name="advance",
    )(me, tangents, up1, dn1, up2, dn2, *bgs)

    h2a, h1a = swap(hia, "vec", 2), swap(hia, "vec", 1)
    h2b, h1b = swap(hib, "vec", 2), swap(hib, "vec", 1)
    near = pl.pallas_call(
        gram_own_kernel,
        out_shape=jax.ShapeDtypeStruct((2 * vectors, 2 * vectors * CHUNK), jnp.float32),
        in_specs=[VM] * 4,
        out_specs=VM,
        compiler_params=SMALL,
        name="gram_own",
    )(hia, hib, h1a, h1b)
    lo, near = lax.optimization_barrier((lo, near))
    l2 = lax.ppermute(lo, "vec", [(0, 2), (1, 3)])
    l1 = lax.ppermute(lo, "vec", [(0, 1), (2, 3)])
    h3a, h3b = swap(h2a, "vec", 1), swap(h2b, "vec", 1)
    high = (hia, hib, h1a, h1b, h2a, h2b, h3a, h3b)

    gram = pl.pallas_call(
        gram_kernel,
        out_shape=jax.ShapeDtypeStruct((count, count), jnp.float32),
        in_specs=[SM] + [VM] * 9,
        out_specs=VM,
        scratch_shapes=[pltpu.VMEM((count, count * CHUNK), jnp.float32)],
        compiler_params=SMALL,
        name="gram",
    )(me, near, *high)
    mask, size = 1, lax.axis_size("space")
    while mask < size:
        if 4 * mask >= size:
            gram, l2 = lax.optimization_barrier((gram, l2))
            l3 = lax.ppermute(l2, "vec", [(2, 3), (3, 2)])
        if 2 * mask < size:
            one, two, three = (swap(gram, "space", k) for k in (mask, 2 * mask, 3 * mask))
            gram = (gram + one) + (two + three)
        else:
            gram = gram + swap(gram, "space", mask)
        mask *= 4

    basis, growth = pl.pallas_call(
        functools.partial(final_kernel, 1.0 / cells),
        out_shape=[
            jax.ShapeDtypeStruct(tangents.shape, jnp.float32),
            jax.ShapeDtypeStruct((1, count), jnp.float32),
        ],
        in_specs=[SM] + [VM] * 11,
        out_specs=[VM, VM],
        scratch_shapes=[pltpu.VMEM((count, count, levels), jnp.float32)],
        compiler_params=SMALL,
        name="final",
    )(me, gram, adv, *high[2:], l1, l2, l3)
    return basis, growth.reshape(count)


def solution(mesh):
    in_specs = (P("vec", None, "space", None, None), P(None, None, "space", "vec", None))
    out_specs = (P("vec", None, "space", None, None), P())
    return jax.shard_map(
        on_device, mesh=mesh, in_specs=in_specs, out_specs=out_specs, check_vma=False
    )
```

```python
import functools

import jax
import jax.numpy as jnp
from jax import lax
from jax.experimental import pallas as pl
from jax.experimental.pallas import tpu as pltpu
from jax.sharding import PartitionSpec as P

time_step = 0.1
diffusion = 0.5
VM = pl.BlockSpec(memory_space=pltpu.VMEM)
SM = pl.BlockSpec(memory_space=pltpu.SMEM)
SMALL = pltpu.CompilerParams(vmem_limit_bytes=12 * 1024 * 1024)
PARAMS = pltpu.CompilerParams(vmem_limit_bytes=20 * 1024 * 1024)
PAD = 8
CHUNK = 16


def stage_rows(src, first, bgs, bg_first, alpha, beta, keep, keep_first, rows, vectors, store):
    columns = src.shape[2] - 2 * PAD
    levels = src.shape[3]
    h = beta * time_step
    lane = lax.broadcasted_iota(jnp.int32, (CHUNK, levels), 1)

    def one_row(row, carry):
        at = row + first
        for x in range(0, columns, CHUNK):
            quarter, inner = divmod(x, bgs.shape[3])
            u, v, r, s = (
                bgs[quarter, bg_first + row, f, inner : inner + CHUNK, :].astype(jnp.float32)
                for f in range(4)
            )
            hu, hv, hr, hs = (0.5 * h) * u, (0.5 * h) * v, (0.5 * h) * r, h * s
            lap = diffusion * h
            xn_c, xp_c = lap - hu, lap + hu
            yn_c, yp_c = lap - hv, lap + hv
            zn_c = jnp.where(lane == levels - 1, 0.0, lap - hr)
            zp_c = jnp.where(lane == 0, 0.0, lap + hr)
            mid = beta - 6.0 * lap
            lo = PAD + x
            for vector in range(vectors):
                centers = [src[at, 2 * vector + f, lo : lo + CHUNK, :] for f in range(2)]
                for f in range(2):
                    k = 2 * vector + f
                    c = centers[f]
                    total = xn_c * src[at, k, lo + 1 : lo + 1 + CHUNK, :]
                    total += xp_c * src[at, k, lo - 1 : lo - 1 + CHUNK, :]
                    total += yn_c * src[at + 1, k, lo : lo + CHUNK, :]
                    total += yp_c * src[at - 1, k, lo : lo + CHUNK, :]
                    total += zn_c * pltpu.roll(c, levels - 1, 1)
                    total += zp_c * pltpu.roll(c, 1, 1)
                    total += mid * c
                    if f == 0:
                        total += h * centers[1]
                    else:
                        total -= hs * centers[0]
                    if alpha:
                        total += alpha * keep[row + keep_first, k, lo : lo + CHUNK, :]
                    store(row, vector, f, x, total)
        return carry

    lax.fori_loop(0, rows, one_row, 0, unroll=2)


def wrap(ref, columns):
    ref[:, :, PAD - 1 : PAD, :] = ref[:, :, PAD + columns - 1 : PAD + columns, :]
    ref[:, :, PAD + columns : PAD + columns + 1, :] = ref[:, :, PAD : PAD + 1, :]


def prep_kernel(own, narrow, last, lead):
    vectors, _, rows = own.shape[:3]
    for vector in range(vectors):
        for f in range(2):
            for row in range(rows):
                value = own[vector, f, row].astype(jnp.bfloat16)
                narrow[row, vector, f] = value
                if row == rows - 1:
                    last[vector, f] = value
                if row == 0:
                    lead[vector, f] = value


def edges_kernel(background, up, dn):
    for f in range(4):
        for row in range(2):
            up[row, f] = background[0, f, row]
            dn[row, f] = background[0, f, row]
        up[2, f] = background[1, f, 1]
        dn[2, f] = background[1, f, 0]


def pack_kernel(background, up, dn, packed):
    for f in range(4):
        for row in range(2):
            packed[row, f] = up[row, f]
            packed[2 + row, f] = background[0, f, row]
            packed[4 + row, f] = dn[row, f]
            packed[7 + row, f] = background[1, f, row]
            packed[10 + row, f] = background[2, f, row]
        packed[6, f] = up[2, f]
        packed[9, f] = dn[2, f]


def advance_kernel(me, own, up1, dn1, up2, dn2, bg0, bg1, bg2, bg3, adv, hia, hib, lo, p0, p1, p2, bg):
    vectors, _, rows, columns, _ = own.shape
    for mask, part in enumerate((bg0, bg1, bg2, bg3)):
        bg[me[0] ^ mask] = part[...]
    for vector in range(vectors):
        for f in range(2):
            k = 2 * vector + f
            cells = slice(PAD, PAD + columns)
            p0[0, k, cells, :] = up2[vector, f].astype(jnp.float32)
            p0[7, k, cells, :] = dn2[vector, f].astype(jnp.float32)
            for row in range(2):
                p0[1 + row, k, cells, :] = up1[row, vector, f].astype(jnp.float32)
                p0[3 + row, k, cells, :] = own[vector, f, row]
                p0[5 + row, k, cells, :] = dn1[row, vector, f].astype(jnp.float32)
    wrap(p0, columns)

    def to(ref):
        def store(row, vector, f, x, value):
            ref[row, 2 * vector + f, PAD + x : PAD + x + CHUNK, :] = value

        return store

    def to_out(row, vector, f, x, value):
        adv[vector, f, row, x : x + CHUNK, :] = value
        top = value.astype(jnp.bfloat16)
        hi = (hia, hib)[vector // 2]
        hi[vector % 2, f, row, x : x + CHUNK, :] = top
        lo[vector, f, row, x : x + CHUNK, :] = (value - top.astype(jnp.float32)).astype(jnp.bfloat16)

    stage_rows(p0, 1, bg, 0, 0.0, 1.0, None, 0, 6, vectors, to(p1))
    wrap(p1, columns)
    stage_rows(p1, 1, bg, 6, 0.75, 0.25, p0, 2, 4, vectors, to(p2))
    wrap(p2, columns)
    stage_rows(p2, 1, bg, 10, 1.0 / 3.0, 2.0 / 3.0, p0, 3, 2, vectors, to_out)


def stacked(blocks):
    vectors, fields, rows, columns, _ = blocks[0].shape
    parts = []
    for f in range(fields):
        for y in range(rows):
            for x in range(0, columns, CHUNK):
                parts.append(
                    jnp.concatenate(
                        [h[j, f, y, x : x + CHUNK, :] for h in blocks for j in range(vectors)]
                    )
                )
    return jnp.concatenate(parts, 1)


def pairs(left, right):
    full = lax.dot_general(left, right, (((1,), (1,)), ((), ())), preferred_element_type=jnp.float32)
    row = lax.broadcasted_iota(jnp.int32, full.shape, 0)
    lane = lax.broadcasted_iota(jnp.int32, full.shape, 1)
    full = jnp.where(row % CHUNK == lane % CHUNK, full, 0.0)
    return jnp.sum(full.reshape(full.shape[0] // CHUNK, CHUNK, full.shape[1]), axis=1)


def gram_own_kernel(h0a, h0b, h1a, h1b, out):
    flat = stacked((h0a, h0b, h1a, h1b))
    out[...] = pairs(flat, flat)


def gram_kernel(me, near, h0a, h0b, h1a, h1b, h2a, h2b, h3a, h3b, out, lines):
    vectors = 2 * h0a.shape[0]
    count = 4 * vectors
    size = count * CHUNK
    position = me[0]
    flat, other = stacked((h0a, h0b, h1a, h1b)), stacked((h2a, h2b, h3a, h3b))
    cross = pairs(flat, other)
    far = pairs(other, other)
    for b in range(2):
        for j in range(vectors):
            k = b * vectors + j
            lines[pl.ds((position ^ b) * vectors + j, 1), :] = jnp.concatenate(
                [near[k : k + 1, :], cross[k : k + 1, :]], 1
            )
            lines[pl.ds((position ^ (2 + b)) * vectors + j, 1), :] = jnp.concatenate(
                [jnp.zeros_like(far[k : k + 1, :]), far[k : k + 1, :]], 1
            )
    group = lax.broadcasted_iota(jnp.int32, (size, count), 0) // CHUNK
    target = ((group // vectors) ^ position) * vectors + group % vectors
    pick = jnp.where(target == lax.broadcasted_iota(jnp.int32, (size, count), 1), 1.0, 0.0)
    half = jnp.dot(
        lines[...], pick, precision=lax.Precision.HIGHEST, preferred_element_type=jnp.float32
    )
    row = lax.broadcasted_iota(jnp.int32, (count, count), 0) // (2 * vectors)
    lane = lax.broadcasted_iota(jnp.int32, (count, count), 1) // (2 * vectors)
    out[...] = half + jnp.where(row == lane, 0.0, half.T)


def final_kernel(scale, me, gram, own, h1a, h1b, h2a, h2b, h3a, h3b, l1, l2, l3, basis, growth, inv):
    vectors = own.shape[0]
    count = gram.shape[0]
    position = me[0]
    levels = own.shape[4]
    scaled = gram[...] * scale
    left = [jnp.broadcast_to(scaled[:, i : i + 1], (count, levels)) for i in range(count)]
    unit = lax.broadcasted_iota(jnp.int32, (count, levels), 0)
    column = ((unit // vectors) ^ position) * vectors + unit % vectors
    right = [jnp.where(column == i, 1.0, 0.0) for i in range(count)]
    wide = lax.broadcasted_iota(jnp.int32, (1, levels), 1)
    pivots = jnp.ones((1, levels), jnp.float32)
    for k in range(count):
        pivot = left[k][k : k + 1, :]
        pivots = jnp.where(wide == k, pivot, pivots)
        turn = 1.0 / pivot
        line, unit_line = left[k] * turn, right[k] * turn
        for i in range(k + 1, count):
            factor = left[i][k : k + 1, :]
            left[i] = left[i] - factor * line
            right[i] = right[i] - factor * unit_line
        inv[k] = right[k] / jnp.sqrt(pivot)
    growth[...] = (0.5 * jnp.log(pivots))[:, :count]
    for first in range(0, vectors, 2):
        weights = []
        for i in range(first, first + 2):
            line = inv[position * vectors + i]
            weights.append(
                [
                    jnp.broadcast_to(line[j : j + 1, :], (CHUNK, levels))
                    for j in range(count)
                ]
            )
        for f in range(own.shape[1]):
            for y in range(own.shape[2]):

                def tile(t, carry, f=f, y=y, first=first, weights=weights):
                    at = pl.ds(pl.multiple_of(t * CHUNK, CHUNK), CHUNK)
                    values = [own[j, f, y, at, :] for j in range(vectors)]
                    for h, l in (((h1a, h1b), l1), ((h2a, h2b), l2), ((h3a, h3b), l3)):
                        for j in range(vectors):
                            values.append(
                                h[j // 2][j % 2, f, y, at, :].astype(jnp.float32)
                                + l[j, f, y, at, :].astype(jnp.float32)
                            )
                    for i in range(2):
                        parts = [w * value for w, value in zip(weights[i], values)]
                        while len(parts) > 1:
                            parts = [a + b for a, b in zip(parts[::2], parts[1::2])]
                        basis[first + i, f, y, at, :] = parts[0]
                    return carry

                lax.fori_loop(0, own.shape[3] // CHUNK, tile, 0, unroll=2)


def shift(value, axis, step):
    count = lax.axis_size(axis)
    return lax.ppermute(value, axis, [(i, (i + step) % count) for i in range(count)])


def swap(value, axis, mask):
    return lax.ppermute(value, axis, [(i, i ^ mask) for i in range(lax.axis_size(axis))])


def on_device(tangents, background):
    vectors, fields, rows, columns, levels = tangents.shape
    count = vectors * lax.axis_size("vec")
    cells = fields * rows * columns * levels * lax.axis_size("space")
    me = lax.axis_index("vec").astype(jnp.int32).reshape(1)

    row_shape = jax.ShapeDtypeStruct((vectors, fields, columns, levels), jnp.bfloat16)
    narrow, last, lead = pl.pallas_call(
        prep_kernel,
        out_shape=[jax.ShapeDtypeStruct((rows,) + row_shape.shape, jnp.bfloat16), row_shape, row_shape],
        in_specs=[VM],
        out_specs=[VM] * 3,
        compiler_params=SMALL,
        name="prep",
    )(tangents)
    edge = jax.ShapeDtypeStruct((3, 4) + background.shape[3:], jnp.bfloat16)
    bg_up, bg_dn = pl.pallas_call(
        edges_kernel,
        out_shape=[edge, edge],
        in_specs=[VM],
        out_specs=[VM] * 2,
        compiler_params=SMALL,
        name="edges",
    )(background)
    bg_up = shift(bg_up, "space", 1)
    bg_dn = shift(bg_dn, "space", -1)
    narrow, last, lead, bg_up, bg_dn = lax.optimization_barrier((narrow, last, lead, bg_up, bg_dn))
    up1 = shift(narrow, "space", 1)
    dn1 = shift(narrow, "space", -1)
    up2 = shift(last, "space", 2)
    dn2 = shift(lead, "space", -2)
    packed = pl.pallas_call(
        pack_kernel,
        out_shape=jax.ShapeDtypeStruct((12, 4) + background.shape[3:], jnp.bfloat16),
        in_specs=[VM] * 3,
        out_specs=VM,
        compiler_params=SMALL,
        name="pack",
    )(background, bg_up, bg_dn)
    bg2 = swap(packed, "vec", 2)
    near_bg, far_bg, _ = lax.optimization_barrier((packed, bg2, dn2))
    bgs = [packed, swap(near_bg, "vec", 1), bg2, swap(far_bg, "vec", 1)]

    low = jax.ShapeDtypeStruct(tangents.shape, jnp.bfloat16)
    pair = jax.ShapeDtypeStruct((vectors // 2,) + tangents.shape[1:], jnp.bfloat16)
    fields_all = 2 * vectors
    adv, hia, hib, lo = pl.pallas_call(
        advance_kernel,
        out_shape=[jax.ShapeDtypeStruct(tangents.shape, jnp.float32), pair, pair, low],
        in_specs=[SM] + [VM] * 9,
        out_specs=[VM] * 4,
        scratch_shapes=[
            pltpu.VMEM((8, fields_all, columns + 2 * PAD, levels), jnp.float32),
            pltpu.VMEM((6, fields_all, columns + 2 * PAD, levels), jnp.float32),
            pltpu.VMEM((4, fields_all, columns + 2 * PAD, levels), jnp.float32),
            pltpu.VMEM((4,) + packed.shape, jnp.bfloat16),
            ],
        compiler_params=PARAMS,
        name="advance",
    )(me, tangents, up1, dn1, up2, dn2, *bgs)

    h2a, h1a = swap(hia, "vec", 2), swap(hia, "vec", 1)
    h2b, h1b = swap(hib, "vec", 2), swap(hib, "vec", 1)
    near = pl.pallas_call(
        gram_own_kernel,
        out_shape=jax.ShapeDtypeStruct((2 * vectors, 2 * vectors * CHUNK), jnp.float32),
        in_specs=[VM] * 4,
        out_specs=VM,
        compiler_params=SMALL,
        name="gram_own",
    )(hia, hib, h1a, h1b)
    lo, near = lax.optimization_barrier((lo, near))
    l2 = lax.ppermute(lo, "vec", [(0, 2), (1, 3)])
    l1 = lax.ppermute(lo, "vec", [(0, 1), (2, 3)])
    h3a, h3b = swap(h2a, "vec", 1), swap(h2b, "vec", 1)
    high = (hia, hib, h1a, h1b, h2a, h2b, h3a, h3b)

    gram = pl.pallas_call(
        gram_kernel,
        out_shape=jax.ShapeDtypeStruct((count, count), jnp.float32),
        in_specs=[SM] + [VM] * 9,
        out_specs=VM,
        scratch_shapes=[pltpu.VMEM((count, count * CHUNK), jnp.float32)],
        compiler_params=SMALL,
        name="gram",
    )(me, near, *high)
    mask, size = 1, lax.axis_size("space")
    while mask < size:
        if 4 * mask >= size:
            gram, l2 = lax.optimization_barrier((gram, l2))
            l3 = lax.ppermute(l2, "vec", [(2, 3), (3, 2)])
        if 2 * mask < size:
            one, two, three = (swap(gram, "space", k) for k in (mask, 2 * mask, 3 * mask))
            gram = (gram + one) + (two + three)
        else:
            gram = gram + swap(gram, "space", mask)
        mask *= 4

    basis, growth = pl.pallas_call(
        functools.partial(final_kernel, 1.0 / cells),
        out_shape=[
            jax.ShapeDtypeStruct(tangents.shape, jnp.float32),
            jax.ShapeDtypeStruct((1, count), jnp.float32),
        ],
        in_specs=[SM] + [VM] * 11,
        out_specs=[VM, VM],
        scratch_shapes=[pltpu.VMEM((count, count, levels), jnp.float32)],
        compiler_params=SMALL,
        name="final",
    )(me, gram, adv, *high[2:], l1, l2, l3)
    return basis, growth.reshape(count)


def solution(mesh):
    in_specs = (P("vec", None, "space", None, None), P(None, None, "space", "vec", None))
    out_specs = (P("vec", None, "space", None, None), P())
    return jax.shard_map(
        on_device, mesh=mesh, in_specs=in_specs, out_specs=out_specs, check_vma=False
    )
```

```python
import functools

import jax
import jax.numpy as jnp
from jax import lax
from jax.experimental import pallas as pl
from jax.experimental.pallas import tpu as pltpu
from jax.sharding import PartitionSpec as P

time_step = 0.1
diffusion = 0.5
VM = pl.BlockSpec(memory_space=pltpu.VMEM)
SM = pl.BlockSpec(memory_space=pltpu.SMEM)
SMALL = pltpu.CompilerParams(vmem_limit_bytes=12 * 1024 * 1024)
PARAMS = pltpu.CompilerParams(vmem_limit_bytes=20 * 1024 * 1024)
PAD = 8
CHUNK = 16


def stage_rows(src, first, bgs, bg_first, alpha, beta, keep, keep_first, rows, vectors, store):
    columns = src.shape[2] - 2 * PAD
    levels = src.shape[3]
    h = beta * time_step
    lane = lax.broadcasted_iota(jnp.int32, (CHUNK, levels), 1)

    def one_row(row, carry):
        at = row + first
        for x in range(0, columns, CHUNK):
            quarter, inner = divmod(x, bgs.shape[3])
            u, v, r, s = (
                bgs[quarter, bg_first + row, f, inner : inner + CHUNK, :].astype(jnp.float32)
                for f in range(4)
            )
            hu, hv, hr, hs = (0.5 * h) * u, (0.5 * h) * v, (0.5 * h) * r, h * s
            lap = diffusion * h
            xn_c, xp_c = lap - hu, lap + hu
            yn_c, yp_c = lap - hv, lap + hv
            zn_c = jnp.where(lane == levels - 1, 0.0, lap - hr)
            zp_c = jnp.where(lane == 0, 0.0, lap + hr)
            mid = beta - 6.0 * lap
            lo = PAD + x
            for vector in range(vectors):
                centers = [src[at, 2 * vector + f, lo : lo + CHUNK, :] for f in range(2)]
                for f in range(2):
                    k = 2 * vector + f
                    c = centers[f]
                    total = xn_c * src[at, k, lo + 1 : lo + 1 + CHUNK, :]
                    total += xp_c * src[at, k, lo - 1 : lo - 1 + CHUNK, :]
                    total += yn_c * src[at + 1, k, lo : lo + CHUNK, :]
                    total += yp_c * src[at - 1, k, lo : lo + CHUNK, :]
                    total += zn_c * pltpu.roll(c, levels - 1, 1)
                    total += zp_c * pltpu.roll(c, 1, 1)
                    total += mid * c
                    if f == 0:
                        total += h * centers[1]
                    else:
                        total -= hs * centers[0]
                    if alpha:
                        total += alpha * keep[row + keep_first, k, lo : lo + CHUNK, :]
                    store(row, vector, f, x, total)
        return carry

    lax.fori_loop(0, rows, one_row, 0, unroll=2)


def wrap(ref, columns):
    ref[:, :, PAD - 1 : PAD, :] = ref[:, :, PAD + columns - 1 : PAD + columns, :]
    ref[:, :, PAD + columns : PAD + columns + 1, :] = ref[:, :, PAD : PAD + 1, :]


def prep_kernel(own, narrow, last, lead):
    vectors, _, rows = own.shape[:3]
    for vector in range(vectors):
        for f in range(2):
            for row in range(rows):
                value = own[vector, f, row].astype(jnp.bfloat16)
                narrow[row, vector, f] = value
                if row == rows - 1:
                    last[vector, f] = value
                if row == 0:
                    lead[vector, f] = value


def edges_kernel(background, up, dn):
    for f in range(4):
        for row in range(2):
            up[row, f] = background[0, f, row]
            dn[row, f] = background[0, f, row]
        up[2, f] = background[1, f, 1]
        dn[2, f] = background[1, f, 0]


def pack_kernel(background, up, dn, packed):
    for f in range(4):
        for row in range(2):
            packed[row, f] = up[row, f]
            packed[2 + row, f] = background[0, f, row]
            packed[4 + row, f] = dn[row, f]
            packed[7 + row, f] = background[1, f, row]
            packed[10 + row, f] = background[2, f, row]
        packed[6, f] = up[2, f]
        packed[9, f] = dn[2, f]


def advance_kernel(me, own, up1, dn1, up2, dn2, bg0, bg1, bg2, bg3, adv, hia, hib, lo, p0, p1, p2, bg):
    vectors, _, rows, columns, _ = own.shape
    for mask, part in enumerate((bg0, bg1, bg2, bg3)):
        bg[me[0] ^ mask] = part[...]
    for vector in range(vectors):
        for f in range(2):
            k = 2 * vector + f
            cells = slice(PAD, PAD + columns)
            p0[0, k, cells, :] = up2[vector, f].astype(jnp.float32)
            p0[7, k, cells, :] = dn2[vector, f].astype(jnp.float32)
            for row in range(2):
                p0[1 + row, k, cells, :] = up1[row, vector, f].astype(jnp.float32)
                p0[3 + row, k, cells, :] = own[vector, f, row]
                p0[5 + row, k, cells, :] = dn1[row, vector, f].astype(jnp.float32)
    wrap(p0, columns)

    def to(ref):
        def store(row, vector, f, x, value):
            ref[row, 2 * vector + f, PAD + x : PAD + x + CHUNK, :] = value

        return store

    def to_out(row, vector, f, x, value):
        adv[vector, f, row, x : x + CHUNK, :] = value
        top = value.astype(jnp.bfloat16)
        hi = (hia, hib)[vector // 2]
        hi[vector % 2, f, row, x : x + CHUNK, :] = top
        lo[vector, f, row, x : x + CHUNK, :] = (value - top.astype(jnp.float32)).astype(jnp.bfloat16)

    stage_rows(p0, 1, bg, 0, 0.0, 1.0, None, 0, 6, vectors, to(p1))
    wrap(p1, columns)
    stage_rows(p1, 1, bg, 6, 0.75, 0.25, p0, 2, 4, vectors, to(p2))
    wrap(p2, columns)
    stage_rows(p2, 1, bg, 10, 1.0 / 3.0, 2.0 / 3.0, p0, 3, 2, vectors, to_out)


def stacked(blocks):
    vectors, fields, rows, columns, _ = blocks[0].shape
    parts = []
    for f in range(fields):
        for y in range(rows):
            for x in range(0, columns, CHUNK):
                parts.append(
                    jnp.concatenate(
                        [h[j, f, y, x : x + CHUNK, :] for h in blocks for j in range(vectors)]
                    )
                )
    return jnp.concatenate(parts, 1)


def pairs(left, right):
    full = lax.dot_general(left, right, (((1,), (1,)), ((), ())), preferred_element_type=jnp.float32)
    row = lax.broadcasted_iota(jnp.int32, full.shape, 0)
    lane = lax.broadcasted_iota(jnp.int32, full.shape, 1)
    full = jnp.where(row % CHUNK == lane % CHUNK, full, 0.0)
    return jnp.sum(full.reshape(full.shape[0] // CHUNK, CHUNK, full.shape[1]), axis=1)


def gram_own_kernel(h0a, h0b, h1a, h1b, out):
    flat = stacked((h0a, h0b, h1a, h1b))
    out[...] = pairs(flat, flat)


def gram_kernel(me, near, h0a, h0b, h1a, h1b, h2a, h2b, h3a, h3b, out, lines):
    vectors = 2 * h0a.shape[0]
    count = 4 * vectors
    size = count * CHUNK
    position = me[0]
    flat, other = stacked((h0a, h0b, h1a, h1b)), stacked((h2a, h2b, h3a, h3b))
    cross = pairs(flat, other)
    far = pairs(other, other)
    for b in range(2):
        for j in range(vectors):
            k = b * vectors + j
            lines[pl.ds((position ^ b) * vectors + j, 1), :] = jnp.concatenate(
                [near[k : k + 1, :], cross[k : k + 1, :]], 1
            )
            lines[pl.ds((position ^ (2 + b)) * vectors + j, 1), :] = jnp.concatenate(
                [jnp.zeros_like(far[k : k + 1, :]), far[k : k + 1, :]], 1
            )
    group = lax.broadcasted_iota(jnp.int32, (size, count), 0) // CHUNK
    target = ((group // vectors) ^ position) * vectors + group % vectors
    pick = jnp.where(target == lax.broadcasted_iota(jnp.int32, (size, count), 1), 1.0, 0.0)
    half = jnp.dot(
        lines[...], pick, precision=lax.Precision.HIGHEST, preferred_element_type=jnp.float32
    )
    row = lax.broadcasted_iota(jnp.int32, (count, count), 0) // (2 * vectors)
    lane = lax.broadcasted_iota(jnp.int32, (count, count), 1) // (2 * vectors)
    out[...] = half + jnp.where(row == lane, 0.0, half.T)


def final_kernel(scale, me, gram, own, h1a, h1b, h2a, h2b, h3a, h3b, l1, l2, l3, basis, growth, inv):
    vectors = own.shape[0]
    count = gram.shape[0]
    position = me[0]
    levels = own.shape[4]
    scaled = gram[...] * scale
    left = [jnp.broadcast_to(scaled[:, i : i + 1], (count, levels)) for i in range(count)]
    unit = lax.broadcasted_iota(jnp.int32, (count, levels), 0)
    column = ((unit // vectors) ^ position) * vectors + unit % vectors
    right = [jnp.where(column == i, 1.0, 0.0) for i in range(count)]
    wide = lax.broadcasted_iota(jnp.int32, (1, levels), 1)
    pivots = jnp.ones((1, levels), jnp.float32)
    for k in range(count):
        pivot = left[k][k : k + 1, :]
        pivots = jnp.where(wide == k, pivot, pivots)
        turn = 1.0 / pivot
        line, unit_line = left[k] * turn, right[k] * turn
        for i in range(k + 1, count):
            factor = left[i][k : k + 1, :]
            left[i] = left[i] - factor * line
            right[i] = right[i] - factor * unit_line
        inv[k] = right[k] / jnp.sqrt(pivot)
    growth[...] = (0.5 * jnp.log(pivots))[:, :count]
    for first in range(0, vectors, 2):
        weights = []
        for i in range(first, first + 2):
            line = inv[position * vectors + i]
            weights.append(
                [
                    jnp.broadcast_to(line[j : j + 1, :], (CHUNK, levels))
                    for j in range(count)
                ]
            )
        for f in range(own.shape[1]):
            for y in range(own.shape[2]):

                def tile(t, carry, f=f, y=y, first=first, weights=weights):
                    at = pl.ds(pl.multiple_of(t * CHUNK, CHUNK), CHUNK)
                    values = [own[j, f, y, at, :] for j in range(vectors)]
                    for h, l in (((h1a, h1b), l1), ((h2a, h2b), l2), ((h3a, h3b), l3)):
                        for j in range(vectors):
                            values.append(
                                h[j // 2][j % 2, f, y, at, :].astype(jnp.float32)
                                + l[j, f, y, at, :].astype(jnp.float32)
                            )
                    for i in range(2):
                        parts = [w * value for w, value in zip(weights[i], values)]
                        while len(parts) > 1:
                            parts = [a + b for a, b in zip(parts[::2], parts[1::2])]
                        basis[first + i, f, y, at, :] = parts[0]
                    return carry

                lax.fori_loop(0, own.shape[3] // CHUNK, tile, 0, unroll=2)


def shift(value, axis, step):
    count = lax.axis_size(axis)
    return lax.ppermute(value, axis, [(i, (i + step) % count) for i in range(count)])


def swap(value, axis, mask):
    return lax.ppermute(value, axis, [(i, i ^ mask) for i in range(lax.axis_size(axis))])


def on_device(tangents, background):
    vectors, fields, rows, columns, levels = tangents.shape
    count = vectors * lax.axis_size("vec")
    cells = fields * rows * columns * levels * lax.axis_size("space")
    me = lax.axis_index("vec").astype(jnp.int32).reshape(1)

    row_shape = jax.ShapeDtypeStruct((vectors, fields, columns, levels), jnp.bfloat16)
    narrow, last, lead = pl.pallas_call(
        prep_kernel,
        out_shape=[jax.ShapeDtypeStruct((rows,) + row_shape.shape, jnp.bfloat16), row_shape, row_shape],
        in_specs=[VM],
        out_specs=[VM] * 3,
        compiler_params=SMALL,
        name="prep",
    )(tangents)
    edge = jax.ShapeDtypeStruct((3, 4) + background.shape[3:], jnp.bfloat16)
    bg_up, bg_dn = pl.pallas_call(
        edges_kernel,
        out_shape=[edge, edge],
        in_specs=[VM],
        out_specs=[VM] * 2,
        compiler_params=SMALL,
        name="edges",
    )(background)
    bg_up = shift(bg_up, "space", 1)
    bg_dn = shift(bg_dn, "space", -1)
    narrow, last, lead, bg_up, bg_dn = lax.optimization_barrier((narrow, last, lead, bg_up, bg_dn))
    up1 = shift(narrow, "space", 1)
    dn1 = shift(narrow, "space", -1)
    up2 = shift(last, "space", 2)
    dn2 = shift(lead, "space", -2)
    packed = pl.pallas_call(
        pack_kernel,
        out_shape=jax.ShapeDtypeStruct((12, 4) + background.shape[3:], jnp.bfloat16),
        in_specs=[VM] * 3,
        out_specs=VM,
        compiler_params=SMALL,
        name="pack",
    )(background, bg_up, bg_dn)
    bg2 = swap(packed, "vec", 2)
    far_bg, _ = lax.optimization_barrier((bg2, dn2))
    bgs = [packed, swap(packed, "vec", 1), bg2, swap(far_bg, "vec", 1)]

    low = jax.ShapeDtypeStruct(tangents.shape, jnp.bfloat16)
    pair = jax.ShapeDtypeStruct((vectors // 2,) + tangents.shape[1:], jnp.bfloat16)
    fields_all = 2 * vectors
    adv, hia, hib, lo = pl.pallas_call(
        advance_kernel,
        out_shape=[jax.ShapeDtypeStruct(tangents.shape, jnp.float32), pair, pair, low],
        in_specs=[SM] + [VM] * 9,
        out_specs=[VM] * 4,
        scratch_shapes=[
            pltpu.VMEM((8, fields_all, columns + 2 * PAD, levels), jnp.float32),
            pltpu.VMEM((6, fields_all, columns + 2 * PAD, levels), jnp.float32),
            pltpu.VMEM((4, fields_all, columns + 2 * PAD, levels), jnp.float32),
            pltpu.VMEM((4,) + packed.shape, jnp.bfloat16),
            ],
        compiler_params=PARAMS,
        name="advance",
    )(me, tangents, up1, dn1, up2, dn2, *bgs)

    h2a, h1a = swap(hia, "vec", 2), swap(hia, "vec", 1)
    h2b, h1b = swap(hib, "vec", 2), swap(hib, "vec", 1)
    near = pl.pallas_call(
        gram_own_kernel,
        out_shape=jax.ShapeDtypeStruct((2 * vectors, 2 * vectors * CHUNK), jnp.float32),
        in_specs=[VM] * 4,
        out_specs=VM,
        compiler_params=SMALL,
        name="gram_own",
    )(hia, hib, h1a, h1b)
    lo, near = lax.optimization_barrier((lo, near))
    l2 = lax.ppermute(lo, "vec", [(0, 2), (1, 3)])
    l1 = lax.ppermute(lo, "vec", [(0, 1), (2, 3)])
    h3a, h3b = swap(h2a, "vec", 1), swap(h2b, "vec", 1)
    high = (hia, hib, h1a, h1b, h2a, h2b, h3a, h3b)

    gram = pl.pallas_call(
        gram_kernel,
        out_shape=jax.ShapeDtypeStruct((count, count), jnp.float32),
        in_specs=[SM] + [VM] * 9,
        out_specs=VM,
        scratch_shapes=[pltpu.VMEM((count, count * CHUNK), jnp.float32)],
        compiler_params=SMALL,
        name="gram",
    )(me, near, *high)
    mask, size = 1, lax.axis_size("space")
    while mask < size:
        if 4 * mask >= size:
            gram, l2 = lax.optimization_barrier((gram, l2))
            l3 = lax.ppermute(l2, "vec", [(2, 3), (3, 2)])
        if 2 * mask < size:
            one, two, three = (swap(gram, "space", k) for k in (mask, 2 * mask, 3 * mask))
            gram = (gram + one) + (two + three)
        else:
            gram = gram + swap(gram, "space", mask)
        mask *= 4

    basis, growth = pl.pallas_call(
        functools.partial(final_kernel, 1.0 / cells),
        out_shape=[
            jax.ShapeDtypeStruct(tangents.shape, jnp.float32),
            jax.ShapeDtypeStruct((1, count), jnp.float32),
        ],
        in_specs=[SM] + [VM] * 11,
        out_specs=[VM, VM],
        scratch_shapes=[pltpu.VMEM((count, count, levels), jnp.float32)],
        compiler_params=SMALL,
        name="final",
    )(me, gram, adv, *high[2:], l1, l2, l3)
    return basis, growth.reshape(count)


def solution(mesh):
    in_specs = (P("vec", None, "space", None, None), P(None, None, "space", "vec", None))
    out_specs = (P("vec", None, "space", None, None), P())
    return jax.shard_map(
        on_device, mesh=mesh, in_specs=in_specs, out_specs=out_specs, check_vma=False
    )
```
